256 devices in a mesh: branch: 32 (over x, z), row: 4 (over y), top: 2 (over core).
Axes of the slice: x: 4, y: 4, z: 8, core: 2. Of those that a mesh axis runs over, the one named last changes fastest.
Arguments:
- right_sides: bfloat16 [16, 2097152], P(None, ('branch', 'row', 'top')), may hold values from -6 to 6
- positions: bfloat16 [3, 2097152], P(None, ('branch', 'row', 'top')), may hold values from -2 to 2
- point_order: int32 [2097152], P(('branch', 'row', 'top')), may hold values from 0 to 8191, as said below
- leaf_basis: bfloat16 [32, 2097152], P(None, ('branch', 'row', 'top')), may hold values from -0.75 to 0.75
- transfer: bfloat16 [65024, 1024], P(('branch', 'row', 'top')), may hold values from -0.75 to 0.75
- couple_local: bfloat16 [65024, 6, 1024], P(('branch', 'row', 'top')), may hold values from -0.4375 to 0.4375
- partner_local: int32 [65024, 6], P(('branch', 'row', 'top')), may hold values from 0 to 1023, as said below
- transfer_up: bfloat16 [496, 1024], replicated, may hold values from -0.75 to 0.75
- couple_up: bfloat16 [504, 6, 1024], P('top'), may hold values from -2 to 2
- partner_up: int32 [504, 6], replicated, may hold values from 0 to 503, as said below
- send_list: int32 [256, 8, 16], P(('branch', 'row', 'top')), may hold values from 0 to 127, as said below
- side_list: int32 [256, 2, 32], P(('branch', 'row', 'top')), may hold values from 0 to 127, as said below
- pair_target: int32 [256, 1024], P(('branch', 'row', 'top')), may hold values from 0 to 127, as said below
- pair_source: int32 [256, 1024], P(('branch', 'row', 'top')), may hold values from 0 to 319, as said below
- pair_count: int32 [256], P(('branch', 'row', 'top')), may hold values from 192 to 1024, as said below
Outputs:
- potential: float32 [16, 2097152], P(None, ('branch', 'row', 'top'))
The draws below stay inside these ranges and needn't reach their ends.
Inputs may be any that keep to these rules, and one draw needn't show every extreme that they name: `point_order`: each device's block of 8192 entries is a permutation of its own rows. `partner_local`: A node of level k has exactly 6 distinct partners, none itself, among the 8 * 128 / 2^k level-k nodes of its subtree, numbered member * 128 / 2^k + node. `partner_up`: an upper node has exactly 6 distinct partners, none itself, all of its own level. `send_list`: for each sender and member, 16 distinct leaves of the sender. `side_list`: for each sender and side, 32 distinct leaves of the sender. `pair_target`: local leaves of the device; entries at and beyond the device's count are ignored. `pair_source`: table entries as in the reference program; on every device the first 192 pairs take each received leaf exactly once; the rest name own leaves. `pair_count`: some device has the full 1024 pairs.
All inputs are finite; a program needn't handle non-finite values.
Results may differ from the reference program's by a relative error of at most 0.025.
Values may be sent and summed in bfloat16 or wider, within the bound.
A program may use at most 192 MiB of HBM per device.

```python
import jax
import jax.numpy as jnp
import numpy as np
from jax import lax

LEAF = 64
RANK = 32
NRHS = 16
FAR = 6
SLOT = 16
HALO = 32
LEAVES_PER_CHIP = 128
GROUP = 8
DEVS = 256
PTS_DEV = 8192
POINTS = 2097152
NODES_DEV = 254
UPPER = 504
UPPER_E = 496
NEAR_CAP = 1024
LOCAL_CAP = 832
N_BRANCH = 32
N_ROW = 4
N_TOP = 2


def draw_positions(key, part):
    key = jax.random.fold_in(key, 61)
    leaf_total = POINTS // LEAF
    leaf_index = (jnp.arange(POINTS, dtype=jnp.int32) // LEAF).astype(jnp.float32)
    angle = 6.283185307179586 * leaf_index / leaf_total
    centre = jnp.stack([1.4 * jnp.cos(angle), 1.4 * jnp.sin(angle), 0.4 * jnp.sin(7.0 * angle)])
    offsets = jax.random.uniform(key, (3, POINTS), jnp.float32, -0.6, 0.6)
    return (centre + offsets).astype(jnp.bfloat16)


def draw_point_order(key, part):
    key = jax.random.fold_in(key, 11)
    device_total = POINTS // PTS_DEV
    device_keys = jax.random.split(key, device_total)
    orders = jax.vmap(lambda sub_key: jax.random.permutation(sub_key, PTS_DEV))(device_keys)
    return orders.reshape(POINTS).astype(jnp.int32)


def draw_partner_local(key, part):
    key = jax.random.fold_in(key, 23)
    device_total = POINTS // PTS_DEV
    local_depth = LEAVES_PER_CHIP.bit_length() - 1
    widths = np.concatenate([np.full(LEAVES_PER_CHIP >> level_index, LEAVES_PER_CHIP >> level_index) for level_index in range(local_depth)])
    within = np.concatenate([np.arange(LEAVES_PER_CHIP >> level_index) for level_index in range(local_depth)])
    member = np.arange(device_total) % GROUP
    own_index = jnp.asarray(member[:, None] * widths[None, :] + within[None, :], jnp.int32)
    level_span = jnp.asarray(GROUP * widths, jnp.int32)
    band_width = (level_span - 1) // FAR
    jitter = jax.random.randint(key, (device_total, NODES_DEV, FAR), 0, band_width[None, :, None])
    strides = 1 + jnp.arange(FAR, dtype=jnp.int32)[None, None, :] * band_width[None, :, None] + jitter
    partner = (own_index[:, :, None] + strides) % level_span[None, :, None]
    return partner.reshape(device_total * NODES_DEV, FAR).astype(jnp.int32)


def draw_partner_up(key, part):
    key = jax.random.fold_in(key, 37)
    device_total = POINTS // PTS_DEV
    upper_levels = device_total.bit_length() - 3
    widths = jnp.asarray(np.concatenate([np.full(device_total >> level_index, device_total >> level_index) for level_index in range(upper_levels)]), jnp.int32)
    within = jnp.asarray(np.concatenate([np.arange(device_total >> level_index) for level_index in range(upper_levels)]), jnp.int32)
    starts = jnp.asarray(np.concatenate([np.full(device_total >> level_index, 2 * device_total - 2 * (device_total >> level_index)) for level_index in range(upper_levels)]), jnp.int32)
    band_width = (widths - 1) // FAR
    jitter = jax.random.randint(key, (UPPER, FAR), 0, band_width[:, None])
    strides = 1 + jnp.arange(FAR, dtype=jnp.int32)[None, :] * band_width[:, None] + jitter
    return (starts[:, None] + (within[:, None] + strides) % widths[:, None]).astype(jnp.int32)


def draw_send_list(key, part):
    key = jax.random.fold_in(key, 53)
    device_total = POINTS // PTS_DEV
    band_width = LEAVES_PER_CHIP // SLOT
    jitter = jax.random.randint(key, (device_total, GROUP, SLOT), 0, band_width)
    return (jnp.arange(SLOT, dtype=jnp.int32) * band_width + jitter).astype(jnp.int32)


def draw_side_list(key, part):
    key = jax.random.fold_in(key, 71)
    device_total = POINTS // PTS_DEV
    band_width = LEAVES_PER_CHIP // HALO
    jitter = jax.random.randint(key, (device_total, 2, HALO), 0, band_width)
    return (jnp.arange(HALO, dtype=jnp.int32) * band_width + jitter).astype(jnp.int32)


def pair_tables(key):
    device_total = POINTS // PTS_DEV
    remote = GROUP * SLOT + 2 * HALO
    key_heavy, key_level, key_perm, key_local, key_target = jax.random.split(key, 5)
    heavy_device = jax.random.randint(key_heavy, (), 0, device_total)
    raw_level = jax.random.randint(key_level, (device_total,), 0, 33)
    raw_level = jnp.where(jnp.arange(device_total) == heavy_device, 32, raw_level)
    extra_pairs = LOCAL_CAP * raw_level ** 4 // 1048576
    counts = remote + extra_pairs
    perm_keys = jax.random.split(key_perm, device_total)
    remote_sources = jax.vmap(lambda sub_key: jax.random.permutation(sub_key, remote))(perm_keys) + LEAVES_PER_CHIP
    local_sources = jax.random.randint(key_local, (device_total, NEAR_CAP - remote), 0, LEAVES_PER_CHIP)
    sources = jnp.concatenate([remote_sources.astype(jnp.int32), local_sources.astype(jnp.int32)], axis=1)
    targets = jax.random.randint(key_target, (device_total, NEAR_CAP), 0, LEAVES_PER_CHIP)
    return (targets.astype(jnp.int32), sources.astype(jnp.int32), counts.astype(jnp.int32))


def draw_pair_target(key, part):
    return pair_tables(key)[0]


def draw_pair_source(key, part):
    return pair_tables(key)[1]


def draw_pair_count(key, part):
    return pair_tables(key)[2]


def levels(stream_key, shape, pieces, least, high):
    factor_of = 1.0
    for axis_at, blocks in pieces:
        draws = jax.random.uniform(jax.random.fold_in(jax.random.fold_in(stream_key, 6), axis_at), (blocks,), jnp.float32, least / len(pieces), high / len(pieces))
        factor_of = factor_of * jnp.repeat(jnp.exp(draws), shape[axis_at] // blocks).reshape((-1,) + (1,) * (len(shape) - 1 - axis_at))
    return factor_of


def gaussian(own_key, extent, deviation, reach, cuts=(), held_as=jnp.bfloat16):
    values = deviation * jax.random.normal(own_key, extent, jnp.float32)
    if cuts:
        values = values * levels(own_key, extent, cuts, -0.22, 0.18)
    return jnp.clip(values, -reach, reach).astype(held_as)


def setup_inputs(seed: int = 0) -> dict:
    arg_keys = jax.random.split(jax.random.key(seed), 16)
    return {
        "right_sides": gaussian(arg_keys[0], (NRHS, POINTS), 1.0, 6.0, ((1, 256),)),
        "positions": draw_positions(jax.random.fold_in(arg_keys[15], 71), 0),
        "point_order": draw_point_order(jax.random.fold_in(arg_keys[15], 71), 0),
        "leaf_basis": gaussian(arg_keys[3], (RANK, POINTS), LEAF ** -0.5, 0.75, ((1, 256),)),
        "transfer": gaussian(arg_keys[4], (DEVS * NODES_DEV, RANK * RANK), (2 * RANK) ** -0.5, 0.75, ((0, 256),)),
        "couple_local": gaussian(arg_keys[5], (DEVS * NODES_DEV, FAR, RANK * RANK), (FAR * RANK) ** -0.5, 0.4375, ((0, 256),)),
        "partner_local": draw_partner_local(jax.random.fold_in(arg_keys[15], 71), 0),
        "transfer_up": gaussian(arg_keys[7], (UPPER_E, RANK * RANK), (2 * RANK) ** -0.5, 0.75),
        "couple_up": gaussian(arg_keys[8], (UPPER, FAR, RANK * RANK), (RANK // 4) ** -0.5, 2.0, ((0, 2),)),
        "partner_up": draw_partner_up(jax.random.fold_in(arg_keys[15], 71), 0),
        "send_list": draw_send_list(jax.random.fold_in(arg_keys[15], 71), 0),
        "side_list": draw_side_list(jax.random.fold_in(arg_keys[15], 71), 0),
        "pair_target": draw_pair_target(jax.random.fold_in(arg_keys[15], 71), 0),
        "pair_source": draw_pair_source(jax.random.fold_in(arg_keys[15], 71), 0),
        "pair_count": draw_pair_count(jax.random.fold_in(arg_keys[15], 71), 0),
    }


INV_FOUR_PI = 0.07957747154594767
SOFTENING = 0.01

def rounded(values):
    return lax.optimization_barrier(values.astype(jnp.bfloat16))

def kernel_tiles(target_xyz, source_xyz):
    offsets = target_xyz.astype(jnp.float32)[:, :, :, None] - source_xyz.astype(jnp.float32)[:, :, None, :]
    squared = lax.optimization_barrier(jnp.sum(offsets * offsets, axis=1)) + SOFTENING
    return rounded(INV_FOUR_PI / jnp.sqrt(squared))

def upward(child_nodes, edge_rows):
    child_shape = child_nodes.shape
    edge_matrices = edge_rows.reshape(edge_rows.shape[:-1] + (RANK, RANK)).astype(jnp.float32)
    matrix_product = jnp.einsum('...zpm,...zpo->...zmo', edge_matrices, child_nodes.astype(jnp.float32))
    paired = matrix_product.reshape(child_shape[:-3] + (child_shape[-3] // 2, 2) + child_shape[-2:])
    return rounded(paired[..., 0, :, :] + paired[..., 1, :, :])

def downward(parents, edge_rows, coupled_result):
    edge_matrices = edge_rows.reshape(edge_rows.shape[:-1] + (RANK, RANK)).astype(jnp.float32)
    spread_values = jnp.repeat(rounded(parents), 2, axis=-3).astype(jnp.float32)
    return coupled_result + jnp.einsum('...rjh,...rhs->...rjs', edge_matrices, spread_values)

def reference(right_sides, positions, point_order, leaf_basis, transfer, couple_local, partner_local, transfer_up, couple_up, partner_up, send_list, side_list, pair_target, pair_source, pair_count):
    devices = N_BRANCH * N_ROW * N_TOP
    group_size = N_ROW * N_TOP
    local_depth = LEAVES_PER_CHIP.bit_length() - 1
    upper_levels = devices.bit_length() - 3
    places = jnp.arange(POINTS, dtype=jnp.int32) // PTS_DEV * PTS_DEV + point_order
    ordered = right_sides[:, places]
    leaf_major = ordered.reshape(NRHS, devices, LEAVES_PER_CHIP, LEAF).transpose(1, 2, 0, 3)
    xyz_major = positions.reshape(3, devices, LEAVES_PER_CHIP, LEAF).transpose(1, 2, 0, 3)
    basis_rows = leaf_basis.reshape(RANK, devices, LEAVES_PER_CHIP, LEAF).transpose(1, 0, 2, 3)
    moments = rounded(jnp.einsum('dlnp,drlp->dlrn', leaf_major.astype(jnp.float32), basis_rows.astype(jnp.float32)))
    edge_table = transfer.reshape(devices, NODES_DEV, RANK * RANK)
    stacked = []
    for level_index in range(local_depth):
        level_width = LEAVES_PER_CHIP >> level_index
        offset = 2 * LEAVES_PER_CHIP - 2 * level_width
        stacked.append(moments)
        moments = upward(moments, edge_table[:, offset:offset + level_width])
    upper_moments = [moments[:, 0]]
    for level_index in range(1, upper_levels):
        level_width = devices >> level_index - 1
        offset = 2 * devices - 2 * level_width
        upper_moments.append(upward(upper_moments[-1], transfer_up[offset:offset + level_width]))
    all_moments = jnp.concatenate(upper_moments, axis=0)
    picked = all_moments[partner_up].astype(jnp.float32)
    blocks = couple_up.reshape(UPPER, FAR, RANK, RANK).astype(jnp.float32)
    upper_local = jnp.einsum('ufab,ufbn->uan', blocks, picked)

    def segment_span(level_index):
        level_width = devices >> level_index
        offset = 2 * devices - 2 * level_width
        return upper_local[offset:offset + level_width]
    current = segment_span(upper_levels - 1)
    for level_index in range(upper_levels - 1, 0, -1):
        level_width = devices >> level_index - 1
        offset = 2 * devices - 2 * level_width
        current = downward(current, transfer_up[offset:offset + level_width], segment_span(level_index - 1))
    root_locals = current
    pair_mats = couple_local.reshape(devices, NODES_DEV, FAR, RANK, RANK)
    partners = partner_local.reshape(devices, NODES_DEV, FAR)

    def one_device(device):
        branch_index = device // group_size
        member = device % group_size
        own_pairs = lax.dynamic_index_in_dim(pair_mats, device, 0, keepdims=False)
        partner_list = lax.dynamic_index_in_dim(partners, device, 0, keepdims=False)
        own_edges = lax.dynamic_index_in_dim(edge_table, device, 0, keepdims=False)
        coupled_result = []
        for level_index in range(local_depth):
            level_width = LEAVES_PER_CHIP >> level_index
            offset = 2 * LEAVES_PER_CHIP - 2 * level_width
            group_pool = lax.dynamic_slice_in_dim(stacked[level_index], branch_index * group_size, group_size, 0)
            group_pool = group_pool.reshape(group_size * level_width, RANK, NRHS)
            chosen = group_pool[partner_list[offset:offset + level_width]].astype(jnp.float32)
            coupled_result.append(jnp.einsum('ufab,ufbn->uan', own_pairs[offset:offset + level_width].astype(jnp.float32), chosen))
        current_local = lax.dynamic_slice_in_dim(root_locals, device, 1, 0)
        for level_index in range(local_depth - 1, -1, -1):
            level_width = LEAVES_PER_CHIP >> level_index
            offset = 2 * LEAVES_PER_CHIP - 2 * level_width
            current_local = downward(current_local, own_edges[offset:offset + level_width], coupled_result[level_index])
        own_basis = lax.dynamic_index_in_dim(basis_rows, device, 0, keepdims=False)
        far_part = jnp.einsum('rlp,lrn->lnp', own_basis.astype(jnp.float32), rounded(current_local).astype(jnp.float32))
        own_rhs = lax.dynamic_index_in_dim(leaf_major, device, 0, keepdims=False)
        own_xyz = lax.dynamic_index_in_dim(xyz_major, device, 0, keepdims=False)
        senders = (branch_index * group_size + jnp.arange(group_size, dtype=jnp.int32))[:, None]
        leaves = send_list[senders[:, 0], member]
        got_rhs = leaf_major[senders, leaves].reshape(group_size * SLOT, NRHS, LEAF)
        got_xyz = xyz_major[senders, leaves].reshape(group_size * SLOT, 3, LEAF)
        lower = (branch_index - 1) % N_BRANCH * group_size + member
        upper = (branch_index + 1) % N_BRANCH * group_size + member
        lower_leaves = side_list[lower, 1]
        upper_leaves = side_list[upper, 0]
        side_rhs = jnp.concatenate([leaf_major[lower][lower_leaves], leaf_major[upper][upper_leaves]], axis=0)
        side_xyz = jnp.concatenate([xyz_major[lower][lower_leaves], xyz_major[upper][upper_leaves]], axis=0)
        table_rhs = jnp.concatenate([own_rhs, got_rhs, side_rhs], axis=0)
        table_xyz = jnp.concatenate([own_xyz, got_xyz, side_xyz], axis=0)
        targets = lax.dynamic_index_in_dim(pair_target, device, 0, keepdims=False)
        sources = lax.dynamic_index_in_dim(pair_source, device, 0, keepdims=False)
        count_here = pair_count[device]
        kernel_block = kernel_tiles(own_xyz[targets], table_xyz[sources]).astype(jnp.float32)
        pair_terms = jnp.einsum('jpq,jnq->jnp', kernel_block, table_rhs[sources].astype(jnp.float32))
        live_mask = (jnp.arange(NEAR_CAP, dtype=jnp.int32) < count_here).astype(jnp.float32)
        near_part = jnp.zeros((LEAVES_PER_CHIP, NRHS, LEAF), jnp.float32).at[targets].add(pair_terms * live_mask[:, None, None])
        return (near_part + far_part).transpose(1, 0, 2).reshape(NRHS, PTS_DEV)
    results = lax.map(one_device, jnp.arange(devices, dtype=jnp.int32))
    tree_order = results.transpose(1, 0, 2).reshape(NRHS, POINTS)
    return jnp.zeros((NRHS, POINTS), jnp.float32).at[:, places].set(tree_order)
```

```python
import jax
import jax.numpy as jnp
from jax import lax
from jax.experimental import pallas as pl
from jax.experimental.pallas import tpu as pltpu
from jax.sharding import PartitionSpec as P

LEAF = 64
RANK = 32
NRHS = 16
FAR = 6
SLOT = 16
HALO = 32
LEAVES = 128
POINTS = LEAVES * LEAF
NODES = 2 * LEAVES - 2
GROUP = 8
BRANCHES = 32
UPPER = 504
LEVELS = 7
TILES = 64

INV_FOUR_PI = 0.07957747154594767
SOFTENING = 0.01

BF = jnp.bfloat16
F32 = jnp.float32
I32 = jnp.int32
MESH = pl.DeviceIdType.MESH
VMEM = pl.BlockSpec(memory_space=pltpu.VMEM)
SMEM = pl.BlockSpec(memory_space=pltpu.SMEM)
ANY = pl.BlockSpec(memory_space=pl.ANY)


def dot(a, b):
    return jnp.dot(a, b, preferred_element_type=F32)


def dot_nt(a, b):
    return lax.dot_general(a, b, (((1,), (1,)), ((), ())), preferred_element_type=F32)


def iota(shape, axis):
    return lax.broadcasted_iota(I32, shape, axis)


def first_row(level):
    return 2 * LEAVES - 2 * (LEAVES >> level)


def block_turns(value):
    return [value] + [pltpu.roll(value, 32 * step, 1) for step in range(1, 4)]


def spread_edges(rows_of, put):
    value = rows_of(0)
    shape = value.shape
    owner = (iota(shape, 0) >> 1) & 3
    lane = iota(shape, 1) >> 5
    masks = [(owner == k) & (lane == k) for k in range(4)]
    for g in range(8):
        turns = block_turns(rows_of(g))
        for p in range(4):
            out = jnp.zeros(shape, F32)
            for k in range(4):
                out = jnp.where(masks[k], turns[(k - p) % 4], out)
            put(4 * g + p, out)


def spread_blocks(rows_of, put):
    lane = None
    for g in range(8):
        turns = [block_turns(rows_of(f, g)) for f in range(FAR)]
        if lane is None:
            lane = iota(turns[0][0].shape, 1) >> 5
        for a in range(4):
            pick = [turns[f][(f % 4 - a) % 4] for f in range(FAR)]
            low = jnp.where(
                lane == 0, pick[0], jnp.where(lane == 1, pick[1], jnp.where(lane == 2, pick[2], pick[3]))
            )
            high = jnp.where(lane == 0, pick[4], jnp.where(lane == 1, pick[5], 0.0))
            put(4 * g + a, low, high)


def stack_rows(rows, shape):
    sub = iota(shape, 0)
    out = jnp.zeros(shape, F32)
    for k, row in enumerate(rows):
        out = jnp.where(sub == k, row, out)
    return out


def split_three(value):
    high = value.astype(BF).astype(F32)
    rest = value - high
    middle = rest.astype(BF).astype(F32)
    return high, middle, rest - middle


def source_features(xyz):
    x, y, z = xyz[0:1], xyz[1:2], xyz[2:3]
    high, middle, low = split_three(x * x + y * y + z * z)
    return stack_rows([x, y, z, 1.0, 1.0, 1.0, high, middle, low], (16, xyz.shape[1]))


def target_features(xyz):
    x, y, z = xyz[0:1], xyz[1:2], xyz[2:3]
    high, middle, low = split_three(x * x + y * y + z * z + SOFTENING)
    return stack_rows(
        [-2.0 * x, -2.0 * y, -2.0 * z, high, middle, low, 1.0, 1.0, 1.0], (16, xyz.shape[1])
    )


def leaf_blocks(basis):
    lane = iota(basis.shape, 1) >> 6
    zero = jnp.zeros(basis.shape, basis.dtype)
    return jnp.concatenate([jnp.where(lane == j, basis, zero) for j in range(4)], axis=0)


def exchange_kernel(
    rhs, xyz, order, basis, trans, tup, cup, send_s, side_s,
    table_o, pool_o, upper_o, edges_o, edges_up_o, cup_o,
    x_s, table_s, pool_s, edge_s, tail_s, near_s, side_buf, root_s, roots_s, upper_s, cup_send, cup_recv,
    near_send, near_recv, pool_send, pool_recv, root_send, root_recv, up_send, up_recv, cup_sem, local_sem,
):
    branch = lax.axis_index("branch")
    row = lax.axis_index("row")
    top = lax.axis_index("top")
    me = row * 2 + top
    device = branch * GROUP + me

    def member(index):
        return (branch, index // 2, index % 2)

    def peer(offset):
        return (me + offset) % GROUP

    def cousin(offset):
        return ((branch + offset) % BRANCHES, row, top)

    barrier = pltpu.get_barrier_semaphore()
    for offset in range(1, GROUP):
        pl.semaphore_signal(barrier, inc=1, device_id=member(peer(offset)), device_id_type=MESH)

    def greet(offset, carry):
        pl.semaphore_signal(barrier, inc=1, device_id=cousin(offset), device_id_type=MESH)
        return carry

    lax.fori_loop(1, BRANCHES, greet, 0)

    for low in range(32):
        x_s[16 * low : 16 * low + 16, :] = rhs[:, 256 * low : 256 * low + 256]

    def chunk(c, carry):
        lanes = pl.ds(pl.multiple_of(c * 256, 256), 256)
        index = order[:, lanes]
        hot = (iota((256, 256), 0) == (index & 255)).astype(F32).astype(BF)
        wide = dot(x_s[...], hot)
        part = index >> 8
        ordered = jnp.zeros((16, 256), F32)
        for low in range(32):
            ordered = jnp.where(part == low, wide[16 * low : 16 * low + 16], ordered)
        features = source_features(xyz[:, lanes].astype(F32))
        left = iota((16, 128), 1) < 64
        for half in range(2):
            value = ordered[:, 128 * half : 128 * half + 128]
            extra = features[:, 128 * half : 128 * half + 128]
            table_s[4 * c + 2 * half] = jnp.where(left, value, pltpu.roll(extra, 64, 1)).astype(BF)
            table_s[4 * c + 2 * half + 1] = jnp.where(left, pltpu.roll(value, 64, 1), extra).astype(BF)
        pool_s[c] = dot_nt(ordered.astype(BF), leaf_blocks(basis[:, lanes])).astype(BF)
        return carry

    lax.fori_loop(0, 32, chunk, 0)

    def fill(k, carry):
        for m in range(GROUP):
            near_s[m, k] = table_s[send_s[m, k]]
        return carry

    lax.fori_loop(0, SLOT, fill, 0)

    def fill_side(k, carry):
        for s in range(2):
            side_buf[s, k] = table_s[side_s[s, k]]
        return carry

    lax.fori_loop(0, HALO, fill_side, 0)

    pl.semaphore_wait(barrier, GROUP - 1 + BRANCHES - 1)

    started = []

    def send(src, dst, send_sem, recv_sem, device_id):
        copy = pltpu.make_async_remote_copy(
            src_ref=src, dst_ref=dst, send_sem=send_sem, recv_sem=recv_sem,
            device_id=device_id, device_id_type=MESH,
        )
        copy.start()
        started.append(copy)

    locals_ = []

    def keep(src, dst, sem):
        copy = pltpu.make_async_copy(src, dst, sem)
        copy.start()
        locals_.append(copy)

    for offset in range(1, GROUP):
        send(
            pool_s.at[pl.ds(0, 32)], pool_o.at[me, pl.ds(0, 32)],
            pool_send.at[offset - 1], pool_recv.at[offset - 1], member(peer(offset)),
        )
    for offset in range(1, GROUP):
        send(
            near_s.at[peer(offset)], table_o.at[pl.ds(LEAVES + me * SLOT, SLOT)],
            near_send.at[offset - 1], near_recv.at[offset - 1], member(peer(offset)),
        )
    send(
        side_buf.at[1], table_o.at[pl.ds(2 * LEAVES, HALO)],
        near_send.at[7], near_recv.at[7], cousin(1),
    )
    send(
        side_buf.at[0], table_o.at[pl.ds(2 * LEAVES + HALO, HALO)],
        near_send.at[8], near_recv.at[8], cousin(BRANCHES - 1),
    )
    keep(table_s, table_o.at[pl.ds(0, LEAVES)], local_sem.at[0])
    keep(near_s.at[me], table_o.at[pl.ds(LEAVES + me * SLOT, SLOT)], local_sem.at[1])

    slot = iota((16, 252), 0)
    shape = slot & 7
    base = jnp.where(slot < 8, device, device + 1 - 2 * top)
    node = jnp.full((16, 252), -1, I32)
    for level in range(6):
        node = jnp.where(shape == level, 512 - (512 >> level) + (base >> level), node)
    hot = (iota((16, 252), 1) + 252 * top == node).astype(F32).astype(BF)
    for f in range(FAR):
        chosen = dot(hot, cup[f])
        cup_o[f] = chosen[0:8]
        cup_send[f] = chosen[8:16]
    send(cup_send, cup_recv, cup_sem.at[0], cup_sem.at[1], (branch, row, 1 - top))

    tail_s[...] = jnp.zeros((16, 1024), F32)
    tail_s[0:14, :] = trans[240:254, :].astype(F32)

    def spread(c, carry):
        start = pl.multiple_of(c * 16, 16)

        def put(p, out):
            edge_s[pl.ds(c * 512 + p, 16, stride=32), :] = out

        spread_edges(lambda g: trans[pl.ds(start, 16), 128 * g : 128 * g + 128].astype(F32), put)
        return carry

    lax.fori_loop(0, 15, spread, 0)

    def put_tail(p, out):
        edge_s[pl.ds(15 * 512 + p, 16, stride=32), :] = out

    spread_edges(lambda g: tail_s[:, 128 * g : 128 * g + 128], put_tail)

    def round_edges(c, carry):
        rows = pl.ds(pl.multiple_of(c * 256, 256), 256)
        edges_o[rows, :] = edge_s[rows, :].astype(BF)
        return carry

    lax.fori_loop(0, 32, round_edges, 0)

    tile_of = [first_row(level) // 4 for level in range(LEVELS)]
    for level in range(LEVELS - 2):
        for t in range((LEAVES >> level) // 8):
            child = tile_of[level] + 2 * t
            pair = jnp.concatenate([pool_s[child], pool_s[child + 1]], axis=1)
            rows = (first_row(level) + 8 * t) * 32
            pool_s[tile_of[level + 1] + t] = dot(pair, edges_o[rows : rows + 256, :]).astype(BF)
    rows = first_row(5) * 32
    pool_s[63] = dot(pool_s[62], edges_o[rows : rows + 128, :]).astype(BF)
    rows = first_row(6) * 32
    root = dot(pool_s[63], edges_o[rows : rows + 128, :])
    placed = root
    for k in (0, 1, 3):
        placed = jnp.where(me % 4 == k, pltpu.roll(root, (32 * (k - 2)) % 128, 1), placed)
    root_s[...] = placed.astype(BF)
    for offset in range(1, GROUP):
        send(
            root_s, roots_s.at[me],
            root_send.at[offset - 1], root_recv.at[offset - 1], member(peer(offset)),
        )
    roots_s[me] = root_s[...]
    roots = started[-7:]
    for offset in range(1, GROUP):
        send(
            pool_s.at[pl.ds(32, 32)], pool_o.at[me, pl.ds(32, 32)],
            pool_send.at[offset + 6], pool_recv.at[offset + 6], member(peer(offset)),
        )
    keep(pool_s, pool_o.at[me], local_sem.at[2])

    slot = iota((64, 496), 0)
    want = jnp.where(
        slot < 8,
        8 * branch + slot,
        jnp.where(
            slot < 12,
            248 + 4 * branch + slot,
            jnp.where(slot < 14, 372 + 2 * branch + slot, jnp.where(slot < 16, -1, 432 + slot)),
        ),
    )
    chosen = dot((iota((64, 496), 1) == want).astype(F32).astype(BF), tup[...])

    def put_up(p, out):
        edge_s[pl.ds(p, 64, stride=32), :] = out

    spread_edges(lambda g: chosen[:, 128 * g : 128 * g + 128], put_up)
    edges_up_o[...] = edge_s[0:2048, :].astype(BF)

    for copy in roots:
        copy.wait_recv()
    low = roots_s[0] + roots_s[1] + roots_s[2] + roots_s[3]
    high = roots_s[4] + roots_s[5] + roots_s[6] + roots_s[7]
    upper_s[0] = low
    upper_s[1] = high
    first = dot(jnp.concatenate([low, high], axis=1), edges_up_o[0:256, :]).astype(BF)
    upper_s[2] = first
    second = dot(first, edges_up_o[256:384, :]).astype(BF)
    third = dot(second[:, 0:64], edges_up_o[384:448, :]).astype(BF)
    upper_s[3] = jnp.where(iota((16, 128), 1) < 64, second.astype(F32), third.astype(F32)).astype(BF)

    def spread_up(offset, carry):
        pltpu.make_async_remote_copy(
            src_ref=upper_s, dst_ref=upper_o.at[branch],
            send_sem=up_send.at[offset - 1], recv_sem=up_recv.at[offset - 1],
            device_id=cousin(offset), device_id_type=MESH,
        ).start()
        return carry

    lax.fori_loop(1, BRANCHES, spread_up, 0)
    keep(upper_s, upper_o.at[branch], local_sem.at[3])

    for copy in started:
        copy.wait_send()
        if not any(copy is other for other in roots):
            copy.wait_recv()
    for copy in locals_:
        copy.wait()
    cup_o[...] = cup_o[...] + cup_recv[...]

    def finish(offset, carry):
        pltpu.make_async_remote_copy(
            src_ref=upper_s, dst_ref=upper_o.at[branch],
            send_sem=up_send.at[offset - 1], recv_sem=up_recv.at[offset - 1],
            device_id=cousin(offset), device_id_type=MESH,
        ).wait()
        return carry

    lax.fori_loop(1, BRANCHES, finish, 0)


def exchange(rhs, xyz, order, basis, trans, tup, cup, send_list, side_list):
    shape = jax.ShapeDtypeStruct
    return pl.pallas_call(
        exchange_kernel,
        out_shape=(
            shape((2 * LEAVES + 2 * HALO, 16, 128), BF),
            shape((GROUP, TILES, 16, 128), BF),
            shape((BRANCHES, 4, 16, 128), BF),
            shape((8192, 128), BF),
            shape((2048, 128), BF),
            shape((FAR, 8, 1024), F32),
        ),
        in_specs=[VMEM] * 7 + [SMEM] * 2,
        out_specs=(ANY, ANY, ANY, VMEM, VMEM, VMEM),
        scratch_shapes=[
            pltpu.VMEM((512, 256), BF),
            pltpu.VMEM((LEAVES, 16, 128), BF),
            pltpu.VMEM((TILES, 16, 128), BF),
            pltpu.VMEM((8192, 128), F32),
            pltpu.VMEM((16, 1024), F32),
            pltpu.VMEM((GROUP, SLOT, 16, 128), BF),
            pltpu.VMEM((2, HALO, 16, 128), BF),
            pltpu.VMEM((16, 128), BF),
            pltpu.VMEM((GROUP, 16, 128), BF),
            pltpu.VMEM((4, 16, 128), BF),
            pltpu.VMEM((FAR, 8, 1024), F32),
            pltpu.VMEM((FAR, 8, 1024), F32),
            pltpu.SemaphoreType.DMA((9,)),
            pltpu.SemaphoreType.DMA((9,)),
            pltpu.SemaphoreType.DMA((14,)),
            pltpu.SemaphoreType.DMA((14,)),
            pltpu.SemaphoreType.DMA((7,)),
            pltpu.SemaphoreType.DMA((7,)),
            pltpu.SemaphoreType.DMA((BRANCHES - 1,)),
            pltpu.SemaphoreType.DMA((BRANCHES - 1,)),
            pltpu.SemaphoreType.DMA((2,)),
            pltpu.SemaphoreType.DMA((4,)),
        ],
        compiler_params=pltpu.CompilerParams(
            collective_id=0, has_side_effects=True, vmem_limit_bytes=48 * 1024 * 1024
        ),
        name="exchange",
    )(rhs, xyz, order, basis, trans, tup, cup, send_list, side_list)


def local_kernel(
    order, basis, xyz, table, pool, upper, edges, edges_up, cup, couple, codes, pup, target, source, count,
    out,
    feat_s, goal_s, pool_rep, block_s, tail_s, block_up, upper_s, coupled_s, local_s, near_s, sum_s,
):
    branch = lax.axis_index("branch")
    me = lax.axis_index("row") * 2 + lax.axis_index("top")
    device = branch * GROUP + me
    left = iota((16, 128), 1) < 64
    lane_block = iota((16, 128), 1) >> 5

    def goals(c, carry):
        lanes = pl.ds(pl.multiple_of(c * 256, 256), 256)
        features = target_features(xyz[:, lanes].astype(F32))
        for half in range(2):
            value = features[:, 128 * half : 128 * half + 128]
            turned = pltpu.roll(value, 64, 1)
            goal_s[4 * c + 2 * half] = jnp.where(left, value, turned).astype(BF)
            goal_s[4 * c + 2 * half + 1] = jnp.where(left, turned, value).astype(BF)
        return carry

    lax.fori_loop(0, 32, goals, 0)

    eye = (iota((128, 128), 0) == iota((128, 128), 1)).astype(F32).astype(BF)

    def sources(c, carry):
        first = pltpu.roll(table[2 * c].astype(F32), 64, 1)
        both = jnp.where(left, first, table[2 * c + 1].astype(F32)).astype(BF)
        turned = dot_nt(eye, jnp.concatenate([both] * 8, axis=0)).astype(BF)
        feat_s[2 * c] = turned[0:64]
        feat_s[2 * c + 1] = turned[64:128]
        return carry

    lax.fori_loop(0, 160, sources, 0, unroll=4)

    def clear(t, carry):
        near_s[t] = jnp.zeros((16, 128), F32)
        return carry

    lax.fori_loop(0, LEAVES + 1, clear, 0, unroll=3)

    live = count[0]
    lane16 = (iota((64, 64), 1) >> 4)
    zero = jnp.zeros((16, 128), BF)

    def quad(first):
        at = [source[0, first + i] for i in range(4)]
        to = [target[0, first + i] for i in range(4)]
        f = [feat_s[at[i]][:, 0:64] for i in range(4)]
        lhs = jnp.where(lane16 == 0, f[0], jnp.where(lane16 == 1, f[1], jnp.where(lane16 == 2, f[2], f[3])))
        g = [goal_s[to[i]] for i in range(4)]
        rhs = jnp.concatenate(
            [
                jnp.concatenate([jnp.where(left, g[0], zero), zero], axis=1),
                jnp.concatenate([jnp.where(left, zero, g[1]), zero], axis=1),
                jnp.concatenate([zero, jnp.where(left, g[2], zero)], axis=1),
                jnp.concatenate([zero, jnp.where(left, zero, g[3])], axis=1),
            ],
            axis=0,
        )
        tile = lax.rsqrt(dot(lhs, rhs)).astype(BF)
        values = jnp.concatenate([table[at[i]][:, 0:64] for i in range(4)], axis=0)
        wide = dot(values, tile)
        outs = []
        for i in range(4):
            part = wide[16 * i : 16 * i + 16, 128 * (i // 2) : 128 * (i // 2) + 128]
            goal = jnp.where(first + i < live, to[i], LEAVES)
            outs.append((goal, jnp.where(left if i % 2 == 0 else ~left, part, 0.0)))
        return outs

    def near(c, carry):
        outs = []
        for k in range(4):
            outs += quad(c * 16 + 4 * k)
        for goal, part in outs:
            near_s[goal] = near_s[goal] + part
        return carry

    lax.fori_loop(0, (live + 15) // 16, near, 0)

    tail_s[...] = jnp.zeros((FAR, 16, 1024), F32)
    for f in range(FAR):
        tail_s[f, 0:14, :] = couple[f, 240:254, :].astype(F32)

    def spread(c, carry):
        start = pl.multiple_of(c * 16, 16)

        def put(a, low, high):
            block_s[0, pl.ds(c * 512 + a, 16, stride=32), :] = low
            block_s[1, pl.ds(c * 512 + a, 16, stride=32), :] = high

        spread_blocks(lambda f, g: couple[f, pl.ds(start, 16), 128 * g : 128 * g + 128].astype(F32), put)
        return carry

    lax.fori_loop(0, 15, spread, 0)

    def put_tail(a, low, high):
        block_s[0, pl.ds(15 * 512 + a, 16, stride=32), :] = low
        block_s[1, pl.ds(15 * 512 + a, 16, stride=32), :] = high

    spread_blocks(lambda f, g: tail_s[f, :, 128 * g : 128 * g + 128], put_tail)

    def put_up(a, low, high):
        block_up[0, pl.ds(a, 8, stride=32), :] = low
        block_up[1, pl.ds(a, 8, stride=32), :] = high

    spread_blocks(lambda f, g: cup[f, :, 128 * g : 128 * g + 128], put_up)

    def widen(t, carry):
        turns = [v.astype(BF) for v in block_turns(pool[t].astype(F32))]
        for j in range(4):
            value = turns[(3 - j) % 4]
            for k in range(3):
                value = jnp.where(lane_block == k, turns[(k - j) % 4], value)
            pool_rep[4 * t + j] = value
        return carry

    lax.fori_loop(0, GROUP * TILES, widen, 0, unroll=2)

    def picks_of(pick):
        low = jnp.where(
            lane_block == 0,
            pick[0],
            jnp.where(lane_block == 1, pick[1], jnp.where(lane_block == 2, pick[2], pick[3])),
        )
        high = jnp.where(lane_block == 0, pick[4], jnp.where(lane_block == 1, pick[5], zero))
        return jnp.concatenate([low, high], axis=1)

    def diagonal(wide):
        tiles = []
        for half in range(2):
            tile = wide[64 * half + 48 : 64 * half + 64, 128 * half : 128 * half + 128]
            for j in range(3):
                start = 64 * half + 16 * j
                tile = jnp.where(
                    lane_block == j, wide[start : start + 16, 128 * half : 128 * half + 128], tile
                )
            tiles.append(tile)
        return tiles

    def coupling(c, carry):
        rows = []
        for u in range(8):
            rows.append(picks_of([pool_rep[codes[f, 8 * c + u]] for f in range(FAR)]))
        rows256 = pl.ds(pl.multiple_of(c * 256, 256), 256)
        blocks = jnp.concatenate([block_s[0, rows256, :], block_s[1, rows256, :]], axis=1).astype(BF)
        tiles = diagonal(dot_nt(jnp.concatenate(rows, axis=0), blocks))
        coupled_s[2 * c] = tiles[0]
        coupled_s[2 * c + 1] = tiles[1]
        return carry

    lax.fori_loop(0, 32, coupling, 0)

    def thirds(t, carry):
        tile = jnp.zeros((16, 128), F32)
        for j in range(4):
            tile = jnp.where(
                lane_block == j, pltpu.roll(upper[4 * t + j, 3].astype(F32), (32 * (j - 2)) % 128, 1), tile
            )
        upper_s[t] = tile.astype(BF)
        return carry

    lax.fori_loop(0, 8, thirds, 0)
    for t in range(4):
        pair = jnp.concatenate([upper_s[2 * t], upper_s[2 * t + 1]], axis=1)
        upper_s[8 + t] = dot(pair, edges_up[512 + 256 * t : 768 + 256 * t, :]).astype(BF)
    for t in range(2):
        pair = jnp.concatenate([upper_s[8 + 2 * t], upper_s[9 + 2 * t]], axis=1)
        upper_s[12 + t] = dot(pair, edges_up[1536 + 256 * t : 1792 + 256 * t, :]).astype(BF)

    def everywhere(tile, block):
        only = jnp.where(lane_block == block, tile, 0.0)
        only = only + pltpu.roll(only, 32, 1)
        return only + pltpu.roll(only, 64, 1)

    rows = []
    for level in range(6):
        node = 512 - (512 >> level) + (device >> level)
        pick = []
        for f in range(FAR):
            q = pup[f, node] - (512 - (512 >> level))
            if level == 0:
                tile, block = upper[q >> 3, (q >> 2) & 1], q & 3
            elif level == 1:
                tile, block = upper[q >> 2, 2], q & 3
            elif level == 2:
                tile, block = upper[q >> 1, 3], q & 1
            elif level == 3:
                tile, block = upper[q, 3], 2
            else:
                tile, block = upper_s[(8 if level == 4 else 12) + (q >> 2)], q & 3
            pick.append(everywhere(tile.astype(F32), block).astype(BF))
        rows.append(picks_of(pick))
    rows += [jnp.zeros((16, 256), BF)] * 2
    tiles = diagonal(dot_nt(jnp.concatenate(rows, axis=0), jnp.concatenate([block_up[0], block_up[1]], axis=1).astype(BF)))
    edge_rows = [me, 8 + (me >> 1), 12 + (me >> 2), 16 + branch, 48 + (branch >> 1)]
    current = everywhere(tiles[1], 1)
    for level in range(4, -1, -1):
        matrix = edges_up[pl.ds(pl.multiple_of(edge_rows[level] * 32, 32), 32), :]
        step = dot_nt(current.astype(BF), jnp.concatenate([matrix] * 4, axis=0))
        current = everywhere(tiles[level // 4], level % 4) + step

    rows6 = first_row(6) * 32
    local_s[63] = coupled_s[63] + dot_nt(current.astype(BF), edges[rows6 : rows6 + 128, :])
    rows5 = first_row(5) * 32
    local_s[62] = coupled_s[62] + dot_nt(local_s[63].astype(BF), edges[rows5 : rows5 + 128, :])
    for level in range(LEVELS - 3, -1, -1):
        parent = first_row(level + 1) // 4
        child = first_row(level) // 4
        for t in range((LEAVES >> level) // 8):
            start = (first_row(level) + 8 * t) * 32
            wide = dot_nt(local_s[parent + t].astype(BF), edges[start : start + 256, :])
            local_s[child + 2 * t] = coupled_s[child + 2 * t] + wide[:, 0:128]
            local_s[child + 2 * t + 1] = coupled_s[child + 2 * t + 1] + wide[:, 128:256]

    sum_s[...] = jnp.zeros((512, 256), F32)

    def back(c, carry):
        lanes = pl.ds(pl.multiple_of(c * 256, 256), 256)
        far = dot(local_s[c].astype(BF), leaf_blocks(basis[:, lanes]))
        parts = []
        for half in range(2):
            first = near_s[4 * c + 2 * half]
            second = near_s[4 * c + 2 * half + 1]
            parts.append(
                jnp.where(left, first + pltpu.roll(first, 64, 1), second + pltpu.roll(second, 64, 1))
            )
        total = (far + INV_FOUR_PI * jnp.concatenate(parts, axis=1)).astype(BF)
        index = order[:, lanes]
        part = index >> 8
        rows = jnp.concatenate(
            [jnp.where(part == low, total, jnp.zeros((16, 256), BF)) for low in range(32)], axis=0
        )
        hot = (iota((256, 256), 0) == (index & 255)).astype(F32).astype(BF)
        sum_s[...] += dot_nt(rows, hot)
        return carry

    lax.fori_loop(0, 32, back, 0)
    for low in range(32):
        out[:, 256 * low : 256 * low + 256] = sum_s[16 * low : 16 * low + 16, :]


def local(order, basis, xyz, table, pool, upper, edges, edges_up, cup, couple, codes, pup, target, source, count):
    return pl.pallas_call(
        local_kernel,
        out_shape=jax.ShapeDtypeStruct((NRHS, POINTS), F32),
        in_specs=[VMEM] * 10 + [SMEM] * 5,
        out_specs=VMEM,
        scratch_shapes=[
            pltpu.VMEM((2 * LEAVES + 2 * HALO, 64, 128), BF),
            pltpu.VMEM((LEAVES, 16, 128), BF),
            pltpu.VMEM((4 * GROUP * TILES, 16, 128), BF),
            pltpu.VMEM((2, 8192, 128), F32),
            pltpu.VMEM((FAR, 16, 1024), F32),
            pltpu.VMEM((2, 256, 128), F32),
            pltpu.VMEM((14, 16, 128), BF),
            pltpu.VMEM((TILES, 16, 128), F32),
            pltpu.VMEM((TILES, 16, 128), F32),
            pltpu.VMEM((LEAVES + 1, 16, 128), F32),
            pltpu.VMEM((512, 256), F32),
        ],
        compiler_params=pltpu.CompilerParams(vmem_limit_bytes=58 * 1024 * 1024),
        name="local",
    )(order, basis, xyz, table, pool, upper, edges, edges_up, cup, couple, codes, pup, target, source, count)


def body(
    right_sides,
    positions,
    point_order,
    leaf_basis,
    transfer,
    couple_local,
    partner_local,
    transfer_up,
    couple_up,
    partner_up,
    send_list,
    side_list,
    pair_target,
    pair_source,
    pair_count,
):
    order = point_order.reshape(1, POINTS)
    starts = jnp.concatenate(
        [jnp.full((LEAVES >> level,), first_row(level), I32) for level in range(LEVELS)]
    )[None, :]
    widths = jnp.concatenate(
        [jnp.full((LEAVES >> level,), LEVELS - level, I32) for level in range(LEVELS)]
    )[None, :]
    partners = partner_local.T
    codes = (partners >> widths) * 256 + starts + (partners & ((1 << widths) - 1))
    codes = jnp.concatenate([codes, jnp.zeros((FAR, 2), I32)], axis=1)
    table, pool, upper, edges, edges_up, cup = exchange(
        right_sides, positions, order, leaf_basis, transfer, transfer_up,
        couple_up.transpose(1, 0, 2), send_list[0], side_list[0],
    )
    return local(
        order, leaf_basis, positions, table, pool.reshape(GROUP * TILES, 16, 128), upper, edges, edges_up, cup,
        couple_local.transpose(1, 0, 2), codes, partner_up.T, pair_target, pair_source, pair_count,
    )


def solution(mesh):
    placed = (
        P(None, ("branch", "row", "top")),
        P(None, ("branch", "row", "top")),
        P(("branch", "row", "top")),
        P(None, ("branch", "row", "top")),
        P(("branch", "row", "top"), None),
        P(("branch", "row", "top"), None, None),
        P(("branch", "row", "top"), None),
        P(),
        P("top", None, None),
        P(),
        P(("branch", "row", "top"), None, None),
        P(("branch", "row", "top"), None, None),
        P(("branch", "row", "top"), None),
        P(("branch", "row", "top"), None),
        P(("branch", "row", "top")),
    )
    return jax.shard_map(
        body,
        mesh=mesh,
        in_specs=placed,
        out_specs=P(None, ("branch", "row", "top")),
        check_vma=False,
    )
```

```python
import jax
import jax.numpy as jnp
from jax import lax
from jax.experimental import pallas as pl
from jax.experimental.pallas import tpu as pltpu
from jax.sharding import PartitionSpec as P

LEAF = 64
RANK = 32
NRHS = 16
FAR = 6
SLOT = 16
HALO = 32
LEAVES = 128
POINTS = LEAVES * LEAF
NODES = 2 * LEAVES - 2
GROUP = 8
BRANCHES = 32
UPPER = 504
LEVELS = 7
TILES = 64

INV_FOUR_PI = 0.07957747154594767
SOFTENING = 0.01

BF = jnp.bfloat16
F32 = jnp.float32
I32 = jnp.int32
MESH = pl.DeviceIdType.MESH
VMEM = pl.BlockSpec(memory_space=pltpu.VMEM)
SMEM = pl.BlockSpec(memory_space=pltpu.SMEM)
HBM = pl.BlockSpec(memory_space=pltpu.HBM)


def dot(a, b):
    return jnp.dot(a, b, preferred_element_type=F32)


def dot_nt(a, b):
    return lax.dot_general(a, b, (((1,), (1,)), ((), ())), preferred_element_type=F32)


def iota(shape, axis):
    return lax.broadcasted_iota(I32, shape, axis)


def first_row(level):
    return 2 * LEAVES - 2 * (LEAVES >> level)


def block_turns(value):
    return [value] + [pltpu.roll(value, 32 * step, 1) for step in range(1, 4)]


def spread_edges(rows_of, put):
    value = rows_of(0)
    shape = value.shape
    owner = (iota(shape, 0) >> 1) & 3
    lane = iota(shape, 1) >> 5
    masks = [(owner == k) & (lane == k) for k in range(4)]
    for g in range(8):
        turns = block_turns(rows_of(g))
        for p in range(4):
            out = jnp.zeros(shape, F32)
            for k in range(4):
                out = jnp.where(masks[k], turns[(k - p) % 4], out)
            put(4 * g + p, out)


def spread_blocks(rows_of, put):
    lane = None
    for g in range(8):
        turns = [block_turns(rows_of(f, g)) for f in range(FAR)]
        if lane is None:
            lane = iota(turns[0][0].shape, 1) >> 5
        for a in range(4):
            pick = [turns[f][(f % 4 - a) % 4] for f in range(FAR)]
            low = jnp.where(
                lane == 0, pick[0], jnp.where(lane == 1, pick[1], jnp.where(lane == 2, pick[2], pick[3]))
            )
            high = jnp.where(lane == 0, pick[4], jnp.where(lane == 1, pick[5], 0.0))
            put(4 * g + a, low, high)


def stack_rows(rows, shape):
    sub = iota(shape, 0)
    out = jnp.zeros(shape, F32)
    for k, row in enumerate(rows):
        out = jnp.where(sub == k, row, out)
    return out


def split_three(value):
    high = value.astype(BF).astype(F32)
    rest = value - high
    middle = rest.astype(BF).astype(F32)
    return high, middle, rest - middle


def source_features(xyz):
    x, y, z = xyz[0:1], xyz[1:2], xyz[2:3]
    high, middle, low = split_three(x * x + y * y + z * z)
    return stack_rows([x, y, z, 1.0, 1.0, 1.0, high, middle, low], (16, xyz.shape[1]))


def target_features(xyz):
    x, y, z = xyz[0:1], xyz[1:2], xyz[2:3]
    high, middle, low = split_three(x * x + y * y + z * z + SOFTENING)
    return stack_rows(
        [-2.0 * x, -2.0 * y, -2.0 * z, high, middle, low, 1.0, 1.0, 1.0], (16, xyz.shape[1])
    )


def leaf_blocks(basis):
    lane = iota(basis.shape, 1) >> 6
    zero = jnp.zeros(basis.shape, basis.dtype)
    return jnp.concatenate([jnp.where(lane == j, basis, zero) for j in range(4)], axis=0)


def exchange_kernel(
    rhs_h, xyz_h, order_h, basis_h, trans_h, tup_h, cup_h, couple_h, partner_h, send_h, side_h,
    table_o, pool_o, upper_o, edges_o, edges_up_o, cup_o, blocks_o, codes_o,
    rhs, xyz, order, basis, trans, tup, cup, couple, partner, send_s, side_s,
    x_s, table_s, pool_s, edge_s, tail_s, near_s, side_buf, root_s, roots_s, upper_s, cup_own, cup_send, cup_recv,
    edges, edges_up, block_s, block_tail, blocks, codes,
    in_sem, near_send, near_recv, core_send, core_recv, ring_send, ring_recv,
    root_send, root_recv, up_send, up_recv, cup_sem, local_sem,
):
    branch = lax.axis_index("branch")
    row = lax.axis_index("row")
    top = lax.axis_index("top")
    me = row * 2 + top
    device = branch * GROUP + me

    held = (rhs, xyz, order, basis, trans, tup, cup, couple, partner, send_s, side_s)
    given = (rhs_h, xyz_h, order_h, basis_h, trans_h, tup_h, cup_h, couple_h, partner_h, send_h, side_h)
    fetched = [pltpu.make_async_copy(a, b, in_sem.at[i]) for i, (a, b) in enumerate(zip(given, held))]
    for i in (0, 2, 1, 3, 9, 10, 4, 5, 6, 7, 8):
        fetched[i].start()

    def member(index):
        return (branch, index // 2, index % 2)

    def peer(offset):
        return (me + offset) % GROUP

    def cousin(offset):
        return ((branch + offset) % BRANCHES, row, top)

    barrier = pltpu.get_barrier_semaphore()
    for offset in range(1, GROUP):
        pl.semaphore_signal(barrier, inc=1, device_id=member(peer(offset)), device_id_type=MESH)

    def greet(offset, carry):
        pl.semaphore_signal(barrier, inc=1, device_id=cousin(offset), device_id_type=MESH)
        return carry

    lax.fori_loop(1, BRANCHES, greet, 0)

    for i in range(4):
        fetched[i].wait()
    for low in range(32):
        x_s[16 * low : 16 * low + 16, :] = rhs[:, 256 * low : 256 * low + 256]
    row_id = iota((256, 256), 0).astype(F32).astype(BF)
    left = iota((16, 128), 1) < 64

    def chunk(c, carry):
        lanes = pl.ds(pl.multiple_of(c * 512, 512), 512)
        index = order[:, lanes]
        fine = jnp.broadcast_to((index & 255).astype(F32), (16, 512)).astype(BF)
        hots = []
        for k in range(2):
            column = jnp.concatenate([fine[:, 256 * k : 256 * k + 256]] * 16, axis=0)
            hots.append(jnp.where(row_id == column, jnp.ones((), BF), jnp.zeros((), BF)))
        wide = dot(x_s[...], jnp.concatenate(hots, axis=1))
        part = jnp.broadcast_to(index >> 8, (16, 512))
        ordered = jnp.zeros((16, 512), F32)
        for low in range(32):
            ordered = jnp.where(part == low, wide[16 * low : 16 * low + 16], ordered)
        features = source_features(xyz[:, lanes].astype(F32))
        for half in range(4):
            value = ordered[:, 128 * half : 128 * half + 128]
            extra = features[:, 128 * half : 128 * half + 128]
            table_s[8 * c + 2 * half] = jnp.where(left, value, pltpu.roll(extra, 64, 1)).astype(BF)
            table_s[8 * c + 2 * half + 1] = jnp.where(left, pltpu.roll(value, 64, 1), extra).astype(BF)
        rounded = ordered.astype(BF)
        columns = basis[:, lanes]
        for k in range(2):
            pool_s[2 * c + k] = dot_nt(
                rounded[:, 256 * k : 256 * k + 256], leaf_blocks(columns[:, 256 * k : 256 * k + 256])
            ).astype(BF)
        return carry

    lax.fori_loop(0, 16, chunk, 0, unroll=2)

    fetched[9].wait()
    fetched[10].wait()

    def fill(k, carry):
        for m in range(GROUP):
            near_s[m, k] = table_s[send_s[m, k]]
        for s in range(2):
            side_buf[s, 2 * k] = table_s[side_s[s, 2 * k]]
            side_buf[s, 2 * k + 1] = table_s[side_s[s, 2 * k + 1]]
        return carry

    lax.fori_loop(0, SLOT, fill, 0)

    pl.semaphore_wait(barrier, GROUP - 1 + BRANCHES - 1)

    sent = []

    def send(src, dst, send_sem, recv_sem, device_id):
        copy = pltpu.make_async_remote_copy(
            src_ref=src, dst_ref=dst, send_sem=send_sem, recv_sem=recv_sem,
            device_id=device_id, device_id_type=MESH,
        )
        copy.start()
        sent.append(copy)
        return copy

    kept = []

    def keep(src, dst, sem):
        copy = pltpu.make_async_copy(src, dst, sem)
        copy.start()
        kept.append(copy)

    partner_core = (branch, row, 1 - top)
    next_row = (branch, (row + 1) % 4, top)
    last_row = (branch, (row + 3) % 4, top)
    before = ((row + 3) % 4) * 2 + top
    after = ((row + 1) % 4) * 2 + top
    across = ((row + 2) % 4) * 2 + top

    def ring_first(p, src):
        tiles = pl.ds(32 * p, 32)
        one = send(src, pool_o.at[me, tiles], ring_send.at[4 * p], ring_recv.at[4 * p], next_row)
        two = send(src, pool_o.at[me, tiles], ring_send.at[4 * p + 1], ring_recv.at[4 * p + 1], last_row)
        core = send(src, pool_o.at[me, tiles], core_send.at[5 * p], core_recv.at[5 * p], partner_core)
        return one, two, core

    def ring_second(p, first):
        tiles = pl.ds(32 * p, 32)
        first[0].wait_recv()
        lower = pl.ds(32 * p, 16)
        three = send(
            pool_o.at[before, lower], pool_o.at[before, lower],
            ring_send.at[4 * p + 2], ring_recv.at[4 * p + 2], next_row,
        )
        a = send(
            pool_o.at[before, tiles], pool_o.at[before, tiles],
            core_send.at[5 * p + 1], core_recv.at[5 * p + 1], partner_core,
        )
        first[1].wait_recv()
        higher = pl.ds(32 * p + 16, 16)
        four = send(
            pool_o.at[after, higher], pool_o.at[after, higher],
            ring_send.at[4 * p + 3], ring_recv.at[4 * p + 3], last_row,
        )
        b = send(
            pool_o.at[after, tiles], pool_o.at[after, tiles],
            core_send.at[5 * p + 2], core_recv.at[5 * p + 2], partner_core,
        )
        return three, four, a, b

    def ring_third(p, second):
        second[0].wait_recv()
        lower = pl.ds(32 * p, 16)
        a = send(
            pool_o.at[across, lower], pool_o.at[across, lower],
            core_send.at[5 * p + 3], core_recv.at[5 * p + 3], partner_core,
        )
        second[1].wait_recv()
        higher = pl.ds(32 * p + 16, 16)
        b = send(
            pool_o.at[across, higher], pool_o.at[across, higher],
            core_send.at[5 * p + 4], core_recv.at[5 * p + 4], partner_core,
        )
        return a, b

    leaves_first = ring_first(0, pool_s.at[pl.ds(0, 32)])
    arriving = [leaves_first[2]]
    for offset in range(1, GROUP):
        arriving.append(
            send(
                near_s.at[peer(offset)], table_o.at[pl.ds(LEAVES + me * SLOT, SLOT)],
                near_send.at[offset - 1], near_recv.at[offset - 1], member(peer(offset)),
            )
        )
    arriving.append(
        send(
            side_buf.at[1], table_o.at[pl.ds(2 * LEAVES, HALO)],
            near_send.at[7], near_recv.at[7], cousin(1),
        )
    )
    arriving.append(
        send(
            side_buf.at[0], table_o.at[pl.ds(2 * LEAVES + HALO, HALO)],
            near_send.at[8], near_recv.at[8], cousin(BRANCHES - 1),
        )
    )
    keep(table_s, table_o.at[pl.ds(0, LEAVES)], local_sem.at[0])
    keep(near_s.at[me], table_o.at[pl.ds(LEAVES + me * SLOT, SLOT)], local_sem.at[1])

    fetched[4].wait()
    tail_s[...] = jnp.zeros((16, 1024), F32)
    tail_s[0:14, :] = trans[240:254, :].astype(F32)

    def spread_one(rows_of, start, part):
        def put(p, out):
            edge_s[part, pl.ds(p, 16, stride=32), :] = out

        spread_edges(rows_of, put)
        edges[pl.ds(start, 512), :] = edge_s[part, 0:512].astype(BF)

    def spread(c, carry):
        for part in range(3):
            start = pl.multiple_of(48 * c + 16 * part, 16)
            spread_one(
                lambda g: trans[pl.ds(start, 16), 128 * g : 128 * g + 128].astype(F32),
                pl.multiple_of(1536 * c + 512 * part, 512), part,
            )
        return carry

    lax.fori_loop(0, 5, spread, 0)
    spread_one(lambda g: tail_s[:, 128 * g : 128 * g + 128], 7680, 0)
    keep(edges, edges_o, local_sem.at[4])

    tile_of = [first_row(level) // 4 for level in range(LEVELS)]
    for level in range(LEVELS - 2):
        for t in range((LEAVES >> level) // 8):
            child = tile_of[level] + 2 * t
            pair = jnp.concatenate([pool_s[child], pool_s[child + 1]], axis=1)
            rows = (first_row(level) + 8 * t) * 32
            pool_s[tile_of[level + 1] + t] = dot(pair, edges[rows : rows + 256, :]).astype(BF)
    rows = first_row(5) * 32
    pool_s[63] = dot(pool_s[62], edges[rows : rows + 128, :]).astype(BF)
    rows = first_row(6) * 32
    root = dot(pool_s[63], edges[rows : rows + 128, :])
    placed = root
    for k in (0, 1, 3):
        placed = jnp.where(me % 4 == k, pltpu.roll(root, (32 * (k - 2)) % 128, 1), placed)
    root_s[...] = placed.astype(BF)
    roots = []
    for offset in range(1, GROUP):
        roots.append(
            send(
                root_s, roots_s.at[me],
                root_send.at[offset - 1], root_recv.at[offset - 1], member(peer(offset)),
            )
        )
    roots_s[me] = root_s[...]
    rest_first = ring_first(1, pool_s.at[pl.ds(32, 32)])
    arriving.append(rest_first[2])
    keep(pool_s, pool_o.at[me], local_sem.at[2])
    leaves_second = ring_second(0, leaves_first)
    arriving += leaves_second[2:]

    fetched[5].wait()
    slot = iota((64, 496), 0)
    want = jnp.where(
        slot < 8,
        8 * branch + slot,
        jnp.where(
            slot < 12,
            248 + 4 * branch + slot,
            jnp.where(slot < 14, 372 + 2 * branch + slot, jnp.where(slot < 16, -1, 432 + slot)),
        ),
    )
    chosen = dot((iota((64, 496), 1) == want).astype(F32).astype(BF), tup[...])

    def put_up(p, out):
        edge_s[0, pl.ds(p, 64, stride=32), :] = out

    spread_edges(lambda g: chosen[:, 128 * g : 128 * g + 128], put_up)
    edges_up[...] = edge_s[0].astype(BF)
    keep(edges_up, edges_up_o, local_sem.at[5])

    for copy in roots:
        copy.wait_recv()
    low = roots_s[0] + roots_s[1] + roots_s[2] + roots_s[3]
    high = roots_s[4] + roots_s[5] + roots_s[6] + roots_s[7]
    upper_s[0] = low
    upper_s[1] = high
    first = dot(jnp.concatenate([low, high], axis=1), edges_up[0:256, :]).astype(BF)
    upper_s[2] = first
    second = dot(first, edges_up[256:384, :]).astype(BF)
    third = dot(second[:, 0:64], edges_up[384:448, :]).astype(BF)
    upper_s[3] = jnp.where(iota((16, 128), 1) < 64, second.astype(F32), third.astype(F32)).astype(BF)

    def spread_up(offset, carry):
        pltpu.make_async_remote_copy(
            src_ref=upper_s, dst_ref=upper_o.at[branch],
            send_sem=up_send.at[offset - 1], recv_sem=up_recv.at[offset - 1],
            device_id=cousin(offset), device_id_type=MESH,
        ).start()
        return carry

    lax.fori_loop(1, BRANCHES, spread_up, 0)
    keep(upper_s, upper_o.at[branch], local_sem.at[3])

    fetched[6].wait()
    slot = iota((16, 252), 0)
    shape = slot & 7
    base = jnp.where(slot < 8, device, device + 1 - 2 * top)
    node = jnp.full((16, 252), -1, I32)
    for level in range(6):
        node = jnp.where(shape == level, 512 - (512 >> level) + (base >> level), node)
    hot = (iota((16, 252), 1) + 252 * top == node).astype(F32).astype(BF)
    for f in range(FAR):
        chosen = dot(hot, cup[f])
        cup_own[f] = chosen[0:8]
        cup_send[f] = chosen[8:16]
    cup_copy = send(cup_send, cup_recv, cup_sem.at[0], cup_sem.at[1], partner_core)

    fetched[8].wait()
    column = iota((FAR, 254), 1)
    width = jnp.full((FAR, 254), 7, I32)
    start = jnp.zeros((FAR, 254), I32)
    for level in range(1, LEVELS):
        width = jnp.where(column >= first_row(level), 7 - level, width)
        start = jnp.where(column >= first_row(level), first_row(level), start)
    codes[:, 254:256] = jnp.zeros((FAR, 2), I32)
    codes[:, 0:254] = (partner[...] >> width) * 256 + start + (partner[...] & ((1 << width) - 1))
    keep(codes, codes_o, local_sem.at[6])

    fetched[7].wait()
    for f in range(FAR):
        block_tail[f] = jnp.zeros((16, 1024), F32)
        block_tail[f, 0:14, :] = couple[f, 240:254, :].astype(F32)

    def couple_one(rows_of, start, part):
        def put(a, low, high):
            block_s[part, 0, pl.ds(a, 16, stride=32), :] = low
            block_s[part, 1, pl.ds(a, 16, stride=32), :] = high

        spread_blocks(rows_of, put)
        blocks[pl.ds(start, 512), 0:128] = block_s[part, 0].astype(BF)
        blocks[pl.ds(start, 512), 128:256] = block_s[part, 1].astype(BF)

    def couple_rows(c, carry):
        start = pl.multiple_of(16 * c, 16)
        couple_one(
            lambda f, g: couple[f, pl.ds(start, 16), 128 * g : 128 * g + 128].astype(F32),
            pl.multiple_of(512 * c, 512), 0,
        )
        return carry

    lax.fori_loop(0, 8, couple_rows, 0)
    rest_second = ring_second(1, rest_first)
    arriving += rest_second[2:]
    arriving += ring_third(0, leaves_second)
    lax.fori_loop(8, 15, couple_rows, 0)
    arriving += ring_third(1, rest_second)
    couple_one(lambda f, g: block_tail[f, :, 128 * g : 128 * g + 128], 7680, 0)
    keep(blocks, blocks_o, local_sem.at[7])

    cup_copy.wait_recv()
    cup_own[...] = cup_own[...] + cup_recv[...]
    keep(cup_own, cup_o, local_sem.at[8])
    for copy in arriving:
        copy.wait_recv()
    for copy in sent:
        copy.wait_send()

    def finish(offset, carry):
        pltpu.make_async_remote_copy(
            src_ref=upper_s, dst_ref=upper_o.at[branch],
            send_sem=up_send.at[offset - 1], recv_sem=up_recv.at[offset - 1],
            device_id=cousin(offset), device_id_type=MESH,
        ).wait()
        return carry

    lax.fori_loop(1, BRANCHES, finish, 0)
    for copy in kept:
        copy.wait()


def exchange(rhs, xyz, order, basis, trans, tup, cup, couple, partner, send_list, side_list):
    shape = jax.ShapeDtypeStruct
    inputs = (rhs, xyz, order, basis, trans, tup, cup, couple, partner, send_list, side_list)
    return pl.pallas_call(
        exchange_kernel,
        out_shape=(
            shape((2 * LEAVES + 2 * HALO, 16, 128), BF),
            shape((GROUP, TILES, 16, 128), BF),
            shape((BRANCHES, 4, 16, 128), BF),
            shape((8192, 128), BF),
            shape((2048, 128), BF),
            shape((FAR, 8, 1024), F32),
            shape((8192, 256), BF),
            shape((FAR, 256), I32),
        ),
        in_specs=[HBM] * 11,
        out_specs=(HBM,) * 8,
        scratch_shapes=[pltpu.VMEM(value.shape, value.dtype) for value in inputs[:9]]
        + [pltpu.SMEM(value.shape, value.dtype) for value in inputs[9:]]
        + [
            pltpu.VMEM((512, 256), BF),
            pltpu.VMEM((LEAVES, 16, 128), BF),
            pltpu.VMEM((TILES, 16, 128), BF),
            pltpu.VMEM((3, 2048, 128), F32),
            pltpu.VMEM((16, 1024), F32),
            pltpu.VMEM((GROUP, SLOT, 16, 128), BF),
            pltpu.VMEM((2, HALO, 16, 128), BF),
            pltpu.VMEM((16, 128), BF),
            pltpu.VMEM((GROUP, 16, 128), BF),
            pltpu.VMEM((4, 16, 128), BF),
            pltpu.VMEM((FAR, 8, 1024), F32),
            pltpu.VMEM((FAR, 8, 1024), F32),
            pltpu.VMEM((FAR, 8, 1024), F32),
            pltpu.VMEM((8192, 128), BF),
            pltpu.VMEM((2048, 128), BF),
            pltpu.VMEM((1, 2, 512, 128), F32),
            pltpu.VMEM((FAR, 16, 1024), F32),
            pltpu.VMEM((8192, 256), BF),
            pltpu.VMEM((FAR, 256), I32),
        ]
        + [
            pltpu.SemaphoreType.DMA((count,))
            for count in (11, 9, 9, 10, 10, 8, 8, 7, 7, BRANCHES - 1, BRANCHES - 1, 2, 9)
        ],
        compiler_params=pltpu.CompilerParams(
            collective_id=0, has_side_effects=True, vmem_limit_bytes=48 * 1024 * 1024
        ),
        name="exchange",
    )(*inputs)


def local_kernel(
    table_h, target_h, source_h, count_h, xyz_h, pool_h, blocks_h, codes_h, upper_h, edges_up_h, cup_h, pup_h,
    edges_h, basis_h, order_h,
    out,
    table, target, source, count, xyz, pool, blocks, codes, upper, edges_up, cup, pup, edges, basis, order,
    swap_s, goal_s, pool_rep, block_up, upper_s, coupled_s, local_s, near_s, sum_s, in_sem,
):
    given = (table_h, target_h, source_h, count_h, xyz_h, pool_h, blocks_h, codes_h, upper_h, edges_up_h, cup_h, pup_h,
             edges_h, basis_h, order_h)
    held = (table, target, source, count, xyz, pool, blocks, codes, upper, edges_up, cup, pup, edges, basis, order)
    fetched = [pltpu.make_async_copy(a, b, in_sem.at[i]) for i, (a, b) in enumerate(zip(given, held))]
    for copy in fetched:
        copy.start()
    for copy in fetched[:5]:
        copy.wait()
    branch = lax.axis_index("branch")
    me = lax.axis_index("row") * 2 + lax.axis_index("top")
    device = branch * GROUP + me
    left = iota((16, 128), 1) < 64
    lane_block = iota((16, 128), 1) >> 5

    eye = (iota((128, 128), 0) == iota((128, 128), 1)).astype(F32).astype(BF)

    def goals(c, carry):
        lanes = pl.ds(pl.multiple_of(c * 128, 128), 128)
        features = target_features(xyz[:, lanes].astype(F32)).astype(BF)
        turned = dot_nt(eye, jnp.concatenate([features] * 4, axis=0)).astype(BF)
        goal_s[2 * c] = turned[0:64]
        goal_s[2 * c + 1] = turned[64:128]
        return carry

    lax.fori_loop(0, 64, goals, 0, unroll=16)

    def swaps(c, carry):
        tiles = table[pl.ds(8 * c, 8)].reshape(128, 128).astype(F32)
        swap_s[pl.ds(8 * c, 8)] = pltpu.roll(tiles, 64, 1).astype(BF).reshape(8, 16, 128)
        return carry

    lax.fori_loop(0, 40, swaps, 0, unroll=4)

    def clear(t, carry):
        near_s[t] = jnp.zeros((16, 64), F32)
        return carry

    lax.fori_loop(0, LEAVES + 1, clear, 0, unroll=3)

    live = count[0]
    lane16 = (iota((64, 64), 1) >> 4)
    zero = jnp.zeros((16, 128), BF)

    def quad(first):
        at = [source[0, first + i] for i in range(4)]
        to = [target[0, first + i] for i in range(4)]
        g = [goal_s[to[i]] for i in range(4)]
        lhs = jnp.where(lane16 == 0, g[0], jnp.where(lane16 == 1, g[1], jnp.where(lane16 == 2, g[2], g[3])))
        value, other = [], []
        for i in range(4):
            plain, swapped = table[at[i]], swap_s[at[i]]
            if i % 2 == 0:
                pieces = [jnp.where(left, plain, zero), jnp.where(left, swapped, zero)]
            else:
                pieces = [jnp.where(left, zero, swapped), jnp.where(left, zero, plain)]
            for rows, piece in zip((value, other), pieces):
                rows.append(jnp.concatenate([piece, zero] if i < 2 else [zero, piece], axis=1))
        tile = lax.rsqrt(dot(lhs, jnp.concatenate(other, axis=0))).astype(BF)
        wide = dot_nt(jnp.concatenate(value, axis=0), tile)
        return [
            (jnp.where(first + i < live, to[i], LEAVES), wide[16 * i : 16 * i + 16]) for i in range(4)
        ]

    def near(c, carry):
        outs = []
        for k in range(16):
            outs += quad(c * 64 + 4 * k)
        for goal, part in outs:
            near_s[goal] = near_s[goal] + part
        return carry

    lax.fori_loop(0, (live + 63) // 64, near, 0)

    for copy in fetched[5:12]:
        copy.wait()

    def put_up(a, low, high):
        block_up[0, pl.ds(a, 8, stride=32), :] = low
        block_up[1, pl.ds(a, 8, stride=32), :] = high

    spread_blocks(lambda f, g: cup[f, :, 128 * g : 128 * g + 128], put_up)

    wide_block = iota((128, 128), 1) >> 5

    def widen(t, carry):
        tiles = pool[pl.ds(8 * t, 8)].reshape(128, 128).astype(F32)
        turns = [v.astype(BF) for v in block_turns(tiles)]
        for j in range(4):
            value = turns[(3 - j) % 4]
            for k in range(3):
                value = jnp.where(wide_block == k, turns[(k - j) % 4], value)
            pool_rep[pl.ds(8 * t, 8), j] = value.reshape(8, 16, 128)
        return carry

    lax.fori_loop(0, GROUP * TILES // 8, widen, 0, unroll=4)

    def picks_of(pick):
        low = jnp.where(
            lane_block == 0,
            pick[0],
            jnp.where(lane_block == 1, pick[1], jnp.where(lane_block == 2, pick[2], pick[3])),
        )
        high = jnp.where(lane_block == 0, pick[4], jnp.where(lane_block == 1, pick[5], zero))
        return jnp.concatenate([low, high], axis=1)

    def diagonal(wide):
        tiles = []
        for half in range(2):
            tile = wide[64 * half + 48 : 64 * half + 64, 128 * half : 128 * half + 128]
            for j in range(3):
                start = 64 * half + 16 * j
                tile = jnp.where(
                    lane_block == j, wide[start : start + 16, 128 * half : 128 * half + 128], tile
                )
            tiles.append(tile)
        return tiles

    def coupling(c, carry):
        rows = []
        for u in range(8):
            rows.append(picks_of([pool_rep[codes[f, 8 * c + u] >> 2, codes[f, 8 * c + u] & 3] for f in range(FAR)]))
        matrices = blocks[pl.ds(pl.multiple_of(c * 256, 256), 256), :]
        tiles = diagonal(dot_nt(jnp.concatenate(rows, axis=0), matrices))
        coupled_s[2 * c] = tiles[0]
        coupled_s[2 * c + 1] = tiles[1]
        return carry

    lax.fori_loop(0, 32, coupling, 0, unroll=4)

    def thirds(t, carry):
        tile = jnp.zeros((16, 128), F32)
        for j in range(4):
            tile = jnp.where(
                lane_block == j, pltpu.roll(upper[4 * t + j, 3].astype(F32), (32 * (j - 2)) % 128, 1), tile
            )
        upper_s[t] = tile.astype(BF)
        return carry

    lax.fori_loop(0, 8, thirds, 0)
    for t in range(4):
        pair = jnp.concatenate([upper_s[2 * t], upper_s[2 * t + 1]], axis=1)
        upper_s[8 + t] = dot(pair, edges_up[512 + 256 * t : 768 + 256 * t, :]).astype(BF)
    for t in range(2):
        pair = jnp.concatenate([upper_s[8 + 2 * t], upper_s[9 + 2 * t]], axis=1)
        upper_s[12 + t] = dot(pair, edges_up[1536 + 256 * t : 1792 + 256 * t, :]).astype(BF)

    def everywhere(tile, block):
        only = jnp.where(lane_block == block, tile, 0.0)
        only = only + pltpu.roll(only, 32, 1)
        return only + pltpu.roll(only, 64, 1)

    rows = []
    for level in range(6):
        node = 512 - (512 >> level) + (device >> level)
        pick = []
        for f in range(FAR):
            q = pup[f, node] - (512 - (512 >> level))
            if level == 0:
                tile, block = upper[q >> 3, (q >> 2) & 1], q & 3
            elif level == 1:
                tile, block = upper[q >> 2, 2], q & 3
            elif level == 2:
                tile, block = upper[q >> 1, 3], q & 1
            elif level == 3:
                tile, block = upper[q, 3], 2
            else:
                tile, block = upper_s[(8 if level == 4 else 12) + (q >> 2)], q & 3
            pick.append(everywhere(tile.astype(F32), block).astype(BF))
        rows.append(picks_of(pick))
    rows += [jnp.zeros((16, 256), BF)] * 2
    tiles = diagonal(dot_nt(jnp.concatenate(rows, axis=0), jnp.concatenate([block_up[0], block_up[1]], axis=1).astype(BF)))
    edge_rows = [me, 8 + (me >> 1), 12 + (me >> 2), 16 + branch, 48 + (branch >> 1)]
    current = everywhere(tiles[1], 1)
    for level in range(4, -1, -1):
        matrix = edges_up[pl.ds(pl.multiple_of(edge_rows[level] * 32, 32), 32), :]
        step = dot_nt(current.astype(BF), jnp.concatenate([matrix] * 4, axis=0))
        current = everywhere(tiles[level // 4], level % 4) + step

    for copy in fetched[12:]:
        copy.wait()
    rows6 = first_row(6) * 32
    local_s[63] = coupled_s[63] + dot_nt(current.astype(BF), edges[rows6 : rows6 + 128, :])
    rows5 = first_row(5) * 32
    local_s[62] = coupled_s[62] + dot_nt(local_s[63].astype(BF), edges[rows5 : rows5 + 128, :])
    for level in range(LEVELS - 3, -1, -1):
        parent = first_row(level + 1) // 4
        child = first_row(level) // 4
        for t in range((LEAVES >> level) // 8):
            start = (first_row(level) + 8 * t) * 32
            wide = dot_nt(local_s[parent + t].astype(BF), edges[start : start + 256, :])
            local_s[child + 2 * t] = coupled_s[child + 2 * t] + wide[:, 0:128]
            local_s[child + 2 * t + 1] = coupled_s[child + 2 * t + 1] + wide[:, 128:256]

    sum_s[...] = jnp.zeros((512, 256), F32)

    def back(c, carry):
        tall, hots = [], []
        lows = []
        for k in range(4):
            lanes = pl.ds(pl.multiple_of((4 * c + k) * 256, 256), 256)
            far = dot(local_s[4 * c + k].astype(BF), leaf_blocks(basis[:, lanes]))
            parts = []
            for half in range(2):
                first = near_s[16 * c + 4 * k + 2 * half]
                second = near_s[16 * c + 4 * k + 2 * half + 1]
                parts += [first, second]
            tall.append((far + INV_FOUR_PI * jnp.concatenate(parts, axis=1)).astype(BF))
            index = order[:, lanes]
            lows.append(jnp.broadcast_to((index >> 8).astype(F32), (16, 256)).astype(BF))
            fine = jnp.broadcast_to((index & 255).astype(F32), (16, 256)).astype(BF)
            fine = jnp.concatenate([fine] * 16, axis=0)
            hots.append(jnp.where(row_id == fine, jnp.ones((), BF), jnp.zeros((), BF)))
        total = jnp.concatenate(tall, axis=1)
        part = jnp.concatenate(lows, axis=1)
        none = jnp.zeros((16, 1024), BF)
        rows = jnp.concatenate(
            [jnp.where(part == jnp.asarray(low, BF), total, none) for low in range(32)], axis=0
        )
        sum_s[...] += dot_nt(rows, jnp.concatenate(hots, axis=1))
        return carry

    row_id = iota((256, 256), 0).astype(F32).astype(BF)
    lax.fori_loop(0, 8, back, 0)
    for low in range(32):
        out[:, 256 * low : 256 * low + 256] = sum_s[16 * low : 16 * low + 16, :]


def local(table, target, source, count, xyz, pool, blocks, codes, upper, edges_up, cup, pup, edges, basis, order):
    inputs = (table, target, source, count, xyz, pool, blocks, codes, upper, edges_up, cup, pup, edges, basis, order)
    scalars = (1, 2, 3, 7, 11)
    return pl.pallas_call(
        local_kernel,
        out_shape=jax.ShapeDtypeStruct((NRHS, POINTS), F32),
        in_specs=[HBM] * 15,
        out_specs=VMEM,
        scratch_shapes=[
            (pltpu.SMEM if i in scalars else pltpu.VMEM)(value.shape, value.dtype) for i, value in enumerate(inputs)
        ]
        + [
            pltpu.VMEM((2 * LEAVES + 2 * HALO, 16, 128), BF),
            pltpu.VMEM((LEAVES, 64, 64), BF),
            pltpu.VMEM((GROUP * TILES, 4, 16, 128), BF),
            pltpu.VMEM((2, 256, 128), F32),
            pltpu.VMEM((14, 16, 128), BF),
            pltpu.VMEM((TILES, 16, 128), F32),
            pltpu.VMEM((TILES, 16, 128), F32),
            pltpu.VMEM((LEAVES + 1, 16, 64), F32),
            pltpu.VMEM((512, 256), F32),
            pltpu.SemaphoreType.DMA((15,)),
        ],
        compiler_params=pltpu.CompilerParams(vmem_limit_bytes=48 * 1024 * 1024),
        name="local",
    )(*inputs)


def body(
    right_sides,
    positions,
    point_order,
    leaf_basis,
    transfer,
    couple_local,
    partner_local,
    transfer_up,
    couple_up,
    partner_up,
    send_list,
    side_list,
    pair_target,
    pair_source,
    pair_count,
):
    order = point_order.reshape(1, POINTS)
    table, pool, upper, edges, edges_up, cup, blocks, codes = exchange(
        right_sides, positions, order, leaf_basis, transfer, transfer_up,
        couple_up.transpose(1, 0, 2), couple_local.transpose(1, 0, 2), partner_local.T, send_list[0], side_list[0],
    )
    return local(
        table, pair_target, pair_source, pair_count, positions, pool.reshape(GROUP * TILES, 16, 128), blocks, codes,
        upper, edges_up, cup, partner_up.T, edges, leaf_basis, order,
    )


def solution(mesh):
    placed = (
        P(None, ("branch", "row", "top")),
        P(None, ("branch", "row", "top")),
        P(("branch", "row", "top")),
        P(None, ("branch", "row", "top")),
        P(("branch", "row", "top"), None),
        P(("branch", "row", "top"), None, None),
        P(("branch", "row", "top"), None),
        P(),
        P("top", None, None),
        P(),
        P(("branch", "row", "top"), None, None),
        P(("branch", "row", "top"), None, None),
        P(("branch", "row", "top"), None),
        P(("branch", "row", "top"), None),
        P(("branch", "row", "top")),
    )
    return jax.shard_map(
        body,
        mesh=mesh,
        in_specs=placed,
        out_specs=P(None, ("branch", "row", "top")),
        check_vma=False,
    )
```

```python
import jax
import jax.numpy as jnp
from jax import lax
from jax.experimental import pallas as pl
from jax.experimental.pallas import tpu as pltpu
from jax.sharding import PartitionSpec as P

LEAF = 64
RANK = 32
NRHS = 16
FAR = 6
SLOT = 16
HALO = 32
LEAVES = 128
POINTS = LEAVES * LEAF
NODES = 2 * LEAVES - 2
GROUP = 8
BRANCHES = 32
UPPER = 504
LEVELS = 7
TILES = 64
PITCH = 33

INV_FOUR_PI = 0.07957747154594767
SOFTENING = 0.01

BF = jnp.bfloat16
F32 = jnp.float32
I32 = jnp.int32
MESH = pl.DeviceIdType.MESH
VMEM = pl.BlockSpec(memory_space=pltpu.VMEM)
SMEM = pl.BlockSpec(memory_space=pltpu.SMEM)
HBM = pl.BlockSpec(memory_space=pltpu.HBM)


def dot(a, b):
    return jnp.dot(a, b, preferred_element_type=F32)


def dot_nt(a, b):
    return lax.dot_general(a, b, (((1,), (1,)), ((), ())), preferred_element_type=F32)


def iota(shape, axis):
    return lax.broadcasted_iota(I32, shape, axis)


def first_row(level):
    return 2 * LEAVES - 2 * (LEAVES >> level)


def block_turns(value):
    return [value] + [pltpu.roll(value, 32 * step, 1) for step in range(1, 4)]


def spread_edges(rows_of, put):
    value = rows_of(0)
    shape = value.shape
    owner = (iota(shape, 0) >> 1) & 3
    lane = iota(shape, 1) >> 5
    masks = [(owner == k) & (lane == k) for k in range(4)]
    for g in range(8):
        turns = block_turns(rows_of(g))
        for p in range(4):
            out = jnp.zeros(shape, F32)
            for k in range(4):
                out = jnp.where(masks[k], turns[(k - p) % 4], out)
            put(4 * g + p, out)


def spread_blocks(rows_of, put):
    lane = None
    for g in range(8):
        turns = [block_turns(rows_of(f, g)) for f in range(FAR)]
        if lane is None:
            lane = iota(turns[0][0].shape, 1) >> 5
        for a in range(4):
            pick = [turns[f][(f % 4 - a) % 4] for f in range(FAR)]
            low = jnp.where(
                lane == 0, pick[0], jnp.where(lane == 1, pick[1], jnp.where(lane == 2, pick[2], pick[3]))
            )
            high = jnp.where(lane == 0, pick[4], jnp.where(lane == 1, pick[5], 0.0))
            put(4 * g + a, low, high)


def stack_rows(rows, shape):
    sub = iota(shape, 0)
    out = jnp.zeros(shape, F32)
    for k, row in enumerate(rows):
        out = jnp.where(sub == k, row, out)
    return out


def split_three(value):
    high = value.astype(BF).astype(F32)
    rest = value - high
    middle = rest.astype(BF).astype(F32)
    return high, middle, rest - middle


def source_features(xyz):
    x, y, z = xyz[0:1], xyz[1:2], xyz[2:3]
    high, middle, low = split_three(x * x + y * y + z * z)
    return stack_rows([x, y, z, 1.0, 1.0, 1.0, high, middle, low], (16, xyz.shape[1]))


def target_features(xyz):
    x, y, z = xyz[0:1], xyz[1:2], xyz[2:3]
    high, middle, low = split_three(x * x + y * y + z * z + SOFTENING)
    return stack_rows(
        [-2.0 * x, -2.0 * y, -2.0 * z, high, middle, low, 1.0, 1.0, 1.0], (16, xyz.shape[1])
    )


def leaf_blocks(basis):
    lane = iota(basis.shape, 1) >> 6
    zero = jnp.zeros(basis.shape, basis.dtype)
    return jnp.concatenate([jnp.where(lane == j, basis, zero) for j in range(4)], axis=0)


def exchange_kernel(
    rhs_h, xyz_h, order_h, basis_h, trans_h, tup_h, cup_h, couple_h, partner_h, send_h, side_h,
    table_o, pool_o, upper_o, edges_o, edges_up_o, cup_o, blocks_o, codes_o,
    rhs, xyz, order, basis, trans, tup, cup, couple, partner, send_s, side_s,
    x_s, table_s, pool_s, edge_s, tail_s, near_s, side_buf, root_s, roots_s, upper_s, cup_own, cup_send, cup_recv,
    edges, edges_up, block_s, block_tail, blocks, codes,
    in_sem, near_send, near_recv, core_send, core_recv, ring_send, ring_recv,
    root_send, root_recv, up_send, up_recv, cup_sem, local_sem,
):
    branch = lax.axis_index("branch")
    row = lax.axis_index("row")
    top = lax.axis_index("top")
    me = row * 2 + top
    device = branch * GROUP + me

    held = (rhs, xyz, order, basis, trans, tup, cup, couple, partner, send_s, side_s)
    given = (rhs_h, xyz_h, order_h, basis_h, trans_h, tup_h, cup_h, couple_h, partner_h, send_h, side_h)
    fetched = [pltpu.make_async_copy(a, b, in_sem.at[i]) for i, (a, b) in enumerate(zip(given, held))]
    for i in (4, 0, 2, 1, 3, 9, 10, 5, 6, 8, 7):
        fetched[i].start()

    def member(index):
        return (branch, index // 2, index % 2)

    def peer(offset):
        return (me + offset) % GROUP

    def cousin(offset):
        return ((branch + offset) % BRANCHES, row, top)

    barrier = pltpu.get_barrier_semaphore()
    for offset in range(1, GROUP):
        pl.semaphore_signal(barrier, inc=1, device_id=member(peer(offset)), device_id_type=MESH)

    def greet(offset, carry):
        pl.semaphore_signal(barrier, inc=1, device_id=cousin(offset), device_id_type=MESH)
        return carry

    lax.fori_loop(1, BRANCHES, greet, 0)

    fetched[4].wait()
    tail_s[...] = jnp.zeros((16, 1024), F32)
    tail_s[0:14, :] = trans[240:254, :].astype(F32)

    def spread_one(rows_of, start, part):
        def put(p, out):
            edge_s[part, pl.ds(p, 16, stride=PITCH), :] = out

        spread_edges(rows_of, put)
        for u in range(16):
            rows = pl.ds(pl.multiple_of(start + 32 * u, 32), 32)
            edges[rows, :] = edge_s[part, PITCH * u : PITCH * u + 32].astype(BF)

    def spread(c, carry):
        for part in range(3):
            start = pl.multiple_of(48 * c + 16 * part, 16)
            spread_one(
                lambda g: trans[pl.ds(start, 16), 128 * g : 128 * g + 128].astype(F32),
                1536 * c + 512 * part, part,
            )
        return carry

    lax.fori_loop(0, 5, spread, 0)
    spread_one(lambda g: tail_s[:, 128 * g : 128 * g + 128], 7680, 0)

    for i in range(4):
        fetched[i].wait()
    for low in range(32):
        x_s[16 * low : 16 * low + 16, :] = rhs[:, 256 * low : 256 * low + 256]
    row_id = iota((256, 256), 0).astype(F32).astype(BF)
    left = iota((16, 128), 1) < 64

    def chunk(c, carry):
        lanes = pl.ds(pl.multiple_of(c * 512, 512), 512)
        index = order[:, lanes]
        fine = jnp.broadcast_to((index & 255).astype(F32), (16, 512)).astype(BF)
        hots = []
        for k in range(2):
            column = jnp.concatenate([fine[:, 256 * k : 256 * k + 256]] * 16, axis=0)
            hots.append(jnp.where(row_id == column, jnp.ones((), BF), jnp.zeros((), BF)))
        wide = dot(x_s[...], jnp.concatenate(hots, axis=1))
        part = jnp.broadcast_to(index >> 8, (16, 512))
        ordered = jnp.zeros((16, 512), F32)
        for low in range(32):
            ordered = jnp.where(part == low, wide[16 * low : 16 * low + 16], ordered)
        features = source_features(xyz[:, lanes].astype(F32))
        for half in range(4):
            value = ordered[:, 128 * half : 128 * half + 128]
            extra = features[:, 128 * half : 128 * half + 128]
            table_s[8 * c + 2 * half] = jnp.where(left, value, pltpu.roll(extra, 64, 1)).astype(BF)
            table_s[8 * c + 2 * half + 1] = jnp.where(left, pltpu.roll(value, 64, 1), extra).astype(BF)
        rounded = ordered.astype(BF)
        columns = basis[:, lanes]
        for k in range(2):
            pool_s[2 * c + k] = dot_nt(
                rounded[:, 256 * k : 256 * k + 256], leaf_blocks(columns[:, 256 * k : 256 * k + 256])
            ).astype(BF)
        return carry

    lax.fori_loop(0, 16, chunk, 0, unroll=2)

    tile_of = [first_row(level) // 4 for level in range(LEVELS)]
    for level in range(LEVELS - 2):
        for t in range((LEAVES >> level) // 8):
            child = tile_of[level] + 2 * t
            pair = jnp.concatenate([pool_s[child], pool_s[child + 1]], axis=1)
            rows = (first_row(level) + 8 * t) * 32
            pool_s[tile_of[level + 1] + t] = dot(pair, edges[rows : rows + 256, :]).astype(BF)
    rows = first_row(5) * 32
    pool_s[63] = dot(pool_s[62], edges[rows : rows + 128, :]).astype(BF)
    rows = first_row(6) * 32
    root = dot(pool_s[63], edges[rows : rows + 128, :])
    placed = root
    for k in (0, 1, 3):
        placed = jnp.where(me % 4 == k, pltpu.roll(root, (32 * (k - 2)) % 128, 1), placed)
    root_s[...] = placed.astype(BF)
    pl.semaphore_wait(barrier, GROUP - 1 + BRANCHES - 1)

    sent = []

    def send(src, dst, send_sem, recv_sem, device_id):
        copy = pltpu.make_async_remote_copy(
            src_ref=src, dst_ref=dst, send_sem=send_sem, recv_sem=recv_sem,
            device_id=device_id, device_id_type=MESH,
        )
        copy.start()
        sent.append(copy)
        return copy

    kept = []

    def keep(src, dst, sem):
        copy = pltpu.make_async_copy(src, dst, sem)
        copy.start()
        kept.append(copy)

    partner_core = (branch, row, 1 - top)
    next_row = (branch, (row + 1) % 4, top)
    last_row = (branch, (row + 3) % 4, top)
    before = ((row + 3) % 4) * 2 + top
    after = ((row + 1) % 4) * 2 + top
    across = ((row + 2) % 4) * 2 + top

    def ring_first(p, src):
        tiles = pl.ds(32 * p, 32)
        one = send(src, pool_o.at[me, tiles], ring_send.at[4 * p], ring_recv.at[4 * p], next_row)
        two = send(src, pool_o.at[me, tiles], ring_send.at[4 * p + 1], ring_recv.at[4 * p + 1], last_row)
        core = send(src, pool_o.at[me, tiles], core_send.at[5 * p], core_recv.at[5 * p], partner_core)
        return one, two, core

    def ring_second(p, first):
        tiles = pl.ds(32 * p, 32)
        first[0].wait_recv()
        lower = pl.ds(32 * p, 16)
        three = send(
            pool_o.at[before, lower], pool_o.at[before, lower],
            ring_send.at[4 * p + 2], ring_recv.at[4 * p + 2], next_row,
        )
        a = send(
            pool_o.at[before, tiles], pool_o.at[before, tiles],
            core_send.at[5 * p + 1], core_recv.at[5 * p + 1], partner_core,
        )
        first[1].wait_recv()
        higher = pl.ds(32 * p + 16, 16)
        four = send(
            pool_o.at[after, higher], pool_o.at[after, higher],
            ring_send.at[4 * p + 3], ring_recv.at[4 * p + 3], last_row,
        )
        b = send(
            pool_o.at[after, tiles], pool_o.at[after, tiles],
            core_send.at[5 * p + 2], core_recv.at[5 * p + 2], partner_core,
        )
        return three, four, a, b

    def ring_third(p, second):
        second[0].wait_recv()
        lower = pl.ds(32 * p, 16)
        a = send(
            pool_o.at[across, lower], pool_o.at[across, lower],
            core_send.at[5 * p + 3], core_recv.at[5 * p + 3], partner_core,
        )
        second[1].wait_recv()
        higher = pl.ds(32 * p + 16, 16)
        b = send(
            pool_o.at[across, higher], pool_o.at[across, higher],
            core_send.at[5 * p + 4], core_recv.at[5 * p + 4], partner_core,
        )
        return a, b

    roots = []
    for offset in range(1, GROUP):
        roots.append(
            send(
                root_s, roots_s.at[me],
                root_send.at[offset - 1], root_recv.at[offset - 1], member(peer(offset)),
            )
        )
    roots_s[me] = root_s[...]
    leaves_first = ring_first(0, pool_s.at[pl.ds(0, 32)])
    arriving = [leaves_first[2]]
    fetched[9].wait()
    fetched[10].wait()

    def fill(k, carry):
        for m in range(GROUP):
            near_s[m, k] = table_s[send_s[m, k]]
        for s in range(2):
            side_buf[s, 2 * k] = table_s[side_s[s, 2 * k]]
            side_buf[s, 2 * k + 1] = table_s[side_s[s, 2 * k + 1]]
        return carry

    lax.fori_loop(0, SLOT, fill, 0)

    for offset in range(1, GROUP):
        arriving.append(
            send(
                near_s.at[peer(offset)], table_o.at[pl.ds(LEAVES + me * SLOT, SLOT)],
                near_send.at[offset - 1], near_recv.at[offset - 1], member(peer(offset)),
            )
        )
    arriving.append(
        send(
            side_buf.at[1], table_o.at[pl.ds(2 * LEAVES, HALO)],
            near_send.at[7], near_recv.at[7], cousin(1),
        )
    )
    arriving.append(
        send(
            side_buf.at[0], table_o.at[pl.ds(2 * LEAVES + HALO, HALO)],
            near_send.at[8], near_recv.at[8], cousin(BRANCHES - 1),
        )
    )
    keep(table_s, table_o.at[pl.ds(0, LEAVES)], local_sem.at[0])
    keep(near_s.at[me], table_o.at[pl.ds(LEAVES + me * SLOT, SLOT)], local_sem.at[1])

    rest_first = ring_first(1, pool_s.at[pl.ds(32, 32)])
    arriving.append(rest_first[2])
    keep(pool_s, pool_o.at[me], local_sem.at[2])
    keep(edges, edges_o, local_sem.at[4])

    fetched[5].wait()
    slot = iota((64, 496), 0)
    want = jnp.where(
        slot < 8,
        8 * branch + slot,
        jnp.where(
            slot < 12,
            248 + 4 * branch + slot,
            jnp.where(slot < 14, 372 + 2 * branch + slot, jnp.where(slot < 16, -1, 432 + slot)),
        ),
    )
    chosen = dot((iota((64, 496), 1) == want).astype(F32).astype(BF), tup[...])

    def put_up(p, out):
        edge_s[0, pl.ds(p, 64, stride=PITCH), :] = out

    spread_edges(lambda g: chosen[:, 128 * g : 128 * g + 128], put_up)
    for u in range(64):
        edges_up[32 * u : 32 * u + 32, :] = edge_s[0, PITCH * u : PITCH * u + 32].astype(BF)
    keep(edges_up, edges_up_o, local_sem.at[5])

    for copy in roots:
        copy.wait_recv()
    low = roots_s[0] + roots_s[1] + roots_s[2] + roots_s[3]
    high = roots_s[4] + roots_s[5] + roots_s[6] + roots_s[7]
    upper_s[0] = low
    upper_s[1] = high
    first = dot(jnp.concatenate([low, high], axis=1), edges_up[0:256, :]).astype(BF)
    upper_s[2] = first
    second = dot(first, edges_up[256:384, :]).astype(BF)
    third = dot(second[:, 0:64], edges_up[384:448, :]).astype(BF)
    upper_s[3] = jnp.where(iota((16, 128), 1) < 64, second.astype(F32), third.astype(F32)).astype(BF)

    def spread_up(offset, carry):
        pltpu.make_async_remote_copy(
            src_ref=upper_s, dst_ref=upper_o.at[branch],
            send_sem=up_send.at[offset - 1], recv_sem=up_recv.at[offset - 1],
            device_id=cousin(offset), device_id_type=MESH,
        ).start()
        return carry

    lax.fori_loop(1, BRANCHES, spread_up, 0)
    keep(upper_s, upper_o.at[branch], local_sem.at[3])

    fetched[6].wait()
    slot = iota((16, 252), 0)
    shape = slot & 7
    base = jnp.where(slot < 8, device, device + 1 - 2 * top)
    node = jnp.full((16, 252), -1, I32)
    for level in range(6):
        node = jnp.where(shape == level, 512 - (512 >> level) + (base >> level), node)
    hot = (iota((16, 252), 1) + 252 * top == node).astype(F32).astype(BF)
    for f in range(FAR):
        chosen = dot(hot, cup[f])
        cup_own[f] = chosen[0:8]
        cup_send[f] = chosen[8:16]
    cup_copy = send(cup_send, cup_recv, cup_sem.at[0], cup_sem.at[1], partner_core)

    fetched[8].wait()
    column = iota((FAR, 254), 1)
    width = jnp.full((FAR, 254), 7, I32)
    start = jnp.zeros((FAR, 254), I32)
    for level in range(1, LEVELS):
        width = jnp.where(column >= first_row(level), 7 - level, width)
        start = jnp.where(column >= first_row(level), first_row(level), start)
    codes[:, 254:256] = jnp.zeros((FAR, 2), I32)
    codes[:, 0:254] = (partner[...] >> width) * 256 + start + (partner[...] & ((1 << width) - 1))
    keep(codes, codes_o, local_sem.at[6])

    leaves_second = ring_second(0, leaves_first)
    arriving += leaves_second[2:]

    fetched[7].wait()
    for f in range(FAR):
        block_tail[f] = jnp.zeros((16, 1024), F32)
        block_tail[f, 0:14, :] = couple[f, 240:254, :].astype(F32)

    def couple_one(rows_of, start, part):
        def put(a, low, high):
            block_s[part, 0, pl.ds(a, 16, stride=PITCH), :] = low
            block_s[part, 1, pl.ds(a, 16, stride=PITCH), :] = high

        spread_blocks(rows_of, put)
        for half in range(2):
            for u in range(16):
                rows = pl.ds(pl.multiple_of(start + 32 * u, 32), 32)
                blocks[rows, 128 * half : 128 * half + 128] = block_s[
                    part, half, PITCH * u : PITCH * u + 32
                ].astype(BF)

    def couple_rows(c, carry):
        start = pl.multiple_of(16 * c, 16)
        couple_one(
            lambda f, g: couple[f, pl.ds(start, 16), 128 * g : 128 * g + 128].astype(F32),
            512 * c, 0,
        )
        return carry

    lax.fori_loop(0, 8, couple_rows, 0)
    lax.fori_loop(8, 15, couple_rows, 0)
    rest_second = ring_second(1, rest_first)
    arriving += rest_second[2:]
    couple_one(lambda f, g: block_tail[f, :, 128 * g : 128 * g + 128], 7680, 0)
    keep(blocks, blocks_o, local_sem.at[7])

    arriving += ring_third(0, leaves_second)
    arriving += ring_third(1, rest_second)
    cup_copy.wait_recv()
    cup_own[...] = cup_own[...] + cup_recv[...]
    keep(cup_own, cup_o, local_sem.at[8])
    for copy in arriving:
        copy.wait_recv()
    for copy in sent:
        copy.wait_send()

    def finish(offset, carry):
        pltpu.make_async_remote_copy(
            src_ref=upper_s, dst_ref=upper_o.at[branch],
            send_sem=up_send.at[offset - 1], recv_sem=up_recv.at[offset - 1],
            device_id=cousin(offset), device_id_type=MESH,
        ).wait()
        return carry

    lax.fori_loop(1, BRANCHES, finish, 0)
    for copy in kept:
        copy.wait()


def exchange(rhs, xyz, order, basis, trans, tup, cup, couple, partner, send_list, side_list):
    shape = jax.ShapeDtypeStruct
    inputs = (rhs, xyz, order, basis, trans, tup, cup, couple, partner, send_list, side_list)
    return pl.pallas_call(
        exchange_kernel,
        out_shape=(
            shape((2 * LEAVES + 2 * HALO, 16, 128), BF),
            shape((GROUP, TILES, 16, 128), BF),
            shape((BRANCHES, 4, 16, 128), BF),
            shape((8192, 128), BF),
            shape((2048, 128), BF),
            shape((FAR, 8, 1024), F32),
            shape((8192, 256), BF),
            shape((FAR, 256), I32),
        ),
        in_specs=[HBM] * 11,
        out_specs=(HBM,) * 8,
        scratch_shapes=[pltpu.VMEM(value.shape, value.dtype) for value in inputs[:9]]
        + [pltpu.SMEM(value.shape, value.dtype) for value in inputs[9:]]
        + [
            pltpu.VMEM((512, 256), BF),
            pltpu.VMEM((LEAVES, 16, 128), BF),
            pltpu.VMEM((TILES, 16, 128), BF),
            pltpu.VMEM((3, 64 * PITCH, 128), F32),
            pltpu.VMEM((16, 1024), F32),
            pltpu.VMEM((GROUP, SLOT, 16, 128), BF),
            pltpu.VMEM((2, HALO, 16, 128), BF),
            pltpu.VMEM((16, 128), BF),
            pltpu.VMEM((GROUP, 16, 128), BF),
            pltpu.VMEM((4, 16, 128), BF),
            pltpu.VMEM((FAR, 8, 1024), F32),
            pltpu.VMEM((FAR, 8, 1024), F32),
            pltpu.VMEM((FAR, 8, 1024), F32),
            pltpu.VMEM((8192, 128), BF),
            pltpu.VMEM((2048, 128), BF),
            pltpu.VMEM((1, 2, 16 * PITCH, 128), F32),
            pltpu.VMEM((FAR, 16, 1024), F32),
            pltpu.VMEM((8192, 256), BF),
            pltpu.VMEM((FAR, 256), I32),
        ]
        + [
            pltpu.SemaphoreType.DMA((count,))
            for count in (11, 9, 9, 10, 10, 8, 8, 7, 7, BRANCHES - 1, BRANCHES - 1, 2, 9)
        ],
        compiler_params=pltpu.CompilerParams(
            collective_id=0, has_side_effects=True, vmem_limit_bytes=64 * 1024 * 1024
        ),
        name="exchange",
    )(*inputs)


def local_kernel(
    table_h, target_h, source_h, count_h, xyz_h, pool_h, blocks_h, codes_h, upper_h, edges_up_h, cup_h, pup_h,
    edges_h, basis_h, order_h,
    out,
    table, target, source, count, xyz, pool, blocks, codes, upper, edges_up, cup, pup, edges, basis, order,
    swap_s, goal_s, pool_rep, block_up, upper_s, coupled_s, local_s, near_s, sum_s, in_sem,
):
    given = (table_h, target_h, source_h, count_h, xyz_h, pool_h, blocks_h, codes_h, upper_h, edges_up_h, cup_h, pup_h,
             edges_h, basis_h, order_h)
    held = (table, target, source, count, xyz, pool, blocks, codes, upper, edges_up, cup, pup, edges, basis, order)
    fetched = [pltpu.make_async_copy(a, b, in_sem.at[i]) for i, (a, b) in enumerate(zip(given, held))]
    for i in (4, 0, 1, 2, 3, 5, 6, 7, 8, 9, 10, 11, 12, 13, 14):
        fetched[i].start()
    fetched[4].wait()
    branch = lax.axis_index("branch")
    me = lax.axis_index("row") * 2 + lax.axis_index("top")
    device = branch * GROUP + me
    left = iota((16, 128), 1) < 64
    lane_block = iota((16, 128), 1) >> 5

    eye = (iota((128, 128), 0) == iota((128, 128), 1)).astype(F32).astype(BF)

    def goals(c, carry):
        lanes = pl.ds(pl.multiple_of(c * 128, 128), 128)
        features = target_features(xyz[:, lanes].astype(F32)).astype(BF)
        turned = dot_nt(eye, jnp.concatenate([features] * 4, axis=0)).astype(BF)
        goal_s[2 * c] = turned[0:64]
        goal_s[2 * c + 1] = turned[64:128]
        return carry

    lax.fori_loop(0, 64, goals, 0, unroll=16)

    def clear(t, carry):
        near_s[t] = jnp.zeros((16, 64), F32)
        return carry

    lax.fori_loop(0, LEAVES + 1, clear, 0, unroll=3)

    for copy in fetched[:4]:
        copy.wait()

    def swaps(c, carry):
        tiles = table[pl.ds(8 * c, 8)].reshape(128, 128).astype(F32)
        swap_s[pl.ds(8 * c, 8)] = pltpu.roll(tiles, 64, 1).astype(BF).reshape(8, 16, 128)
        return carry

    lax.fori_loop(0, 40, swaps, 0, unroll=4)

    live = count[0]
    lane16 = (iota((64, 64), 1) >> 4)
    zero = jnp.zeros((16, 128), BF)

    def quad(first):
        at = [source[0, first + i] for i in range(4)]
        to = [target[0, first + i] for i in range(4)]
        g = [goal_s[to[i]] for i in range(4)]
        lhs = jnp.where(lane16 == 0, g[0], jnp.where(lane16 == 1, g[1], jnp.where(lane16 == 2, g[2], g[3])))
        value, other = [], []
        for i in range(4):
            plain, swapped = table[at[i]], swap_s[at[i]]
            if i % 2 == 0:
                pieces = [jnp.where(left, plain, zero), jnp.where(left, swapped, zero)]
            else:
                pieces = [jnp.where(left, zero, swapped), jnp.where(left, zero, plain)]
            for rows, piece in zip((value, other), pieces):
                rows.append(jnp.concatenate([piece, zero] if i < 2 else [zero, piece], axis=1))
        tile = lax.rsqrt(dot(lhs, jnp.concatenate(other, axis=0))).astype(BF)
        wide = dot_nt(jnp.concatenate(value, axis=0), tile)
        return [
            (jnp.where(first + i < live, to[i], LEAVES), wide[16 * i : 16 * i + 16]) for i in range(4)
        ]

    def near(c, carry):
        outs = []
        for k in range(16):
            outs += quad(c * 64 + 4 * k)
        for goal, part in outs:
            near_s[goal] = near_s[goal] + part
        return carry

    lax.fori_loop(0, (live + 63) // 64, near, 0)

    for copy in fetched[5:12]:
        copy.wait()

    def put_up(a, low, high):
        block_up[0, pl.ds(a, 8, stride=32), :] = low
        block_up[1, pl.ds(a, 8, stride=32), :] = high

    spread_blocks(lambda f, g: cup[f, :, 128 * g : 128 * g + 128], put_up)

    wide_block = iota((128, 128), 1) >> 5

    def widen(t, carry):
        tiles = pool[pl.ds(8 * t, 8)].reshape(128, 128).astype(F32)
        turns = [v.astype(BF) for v in block_turns(tiles)]
        for j in range(4):
            value = turns[(3 - j) % 4]
            for k in range(3):
                value = jnp.where(wide_block == k, turns[(k - j) % 4], value)
            pool_rep[pl.ds(8 * t, 8), j] = value.reshape(8, 16, 128)
        return carry

    lax.fori_loop(0, GROUP * TILES // 8, widen, 0, unroll=4)

    def picks_of(pick):
        low = jnp.where(
            lane_block == 0,
            pick[0],
            jnp.where(lane_block == 1, pick[1], jnp.where(lane_block == 2, pick[2], pick[3])),
        )
        high = jnp.where(lane_block == 0, pick[4], jnp.where(lane_block == 1, pick[5], zero))
        return jnp.concatenate([low, high], axis=1)

    def diagonal(wide):
        tiles = []
        for half in range(2):
            tile = wide[64 * half + 48 : 64 * half + 64, 128 * half : 128 * half + 128]
            for j in range(3):
                start = 64 * half + 16 * j
                tile = jnp.where(
                    lane_block == j, wide[start : start + 16, 128 * half : 128 * half + 128], tile
                )
            tiles.append(tile)
        return tiles

    def coupling(c, carry):
        rows = []
        for u in range(8):
            rows.append(picks_of([pool_rep[codes[f, 8 * c + u] >> 2, codes[f, 8 * c + u] & 3] for f in range(FAR)]))
        matrices = blocks[pl.ds(pl.multiple_of(c * 256, 256), 256), :]
        tiles = diagonal(dot_nt(jnp.concatenate(rows, axis=0), matrices))
        coupled_s[2 * c] = tiles[0]
        coupled_s[2 * c + 1] = tiles[1]
        return carry

    lax.fori_loop(0, 32, coupling, 0, unroll=4)

    def thirds(t, carry):
        tile = jnp.zeros((16, 128), F32)
        for j in range(4):
            tile = jnp.where(
                lane_block == j, pltpu.roll(upper[4 * t + j, 3].astype(F32), (32 * (j - 2)) % 128, 1), tile
            )
        upper_s[t] = tile.astype(BF)
        return carry

    lax.fori_loop(0, 8, thirds, 0)
    for t in range(4):
        pair = jnp.concatenate([upper_s[2 * t], upper_s[2 * t + 1]], axis=1)
        upper_s[8 + t] = dot(pair, edges_up[512 + 256 * t : 768 + 256 * t, :]).astype(BF)
    for t in range(2):
        pair = jnp.concatenate([upper_s[8 + 2 * t], upper_s[9 + 2 * t]], axis=1)
        upper_s[12 + t] = dot(pair, edges_up[1536 + 256 * t : 1792 + 256 * t, :]).astype(BF)

    def everywhere(tile, block):
        only = jnp.where(lane_block == block, tile, 0.0)
        only = only + pltpu.roll(only, 32, 1)
        return only + pltpu.roll(only, 64, 1)

    rows = []
    for level in range(6):
        node = 512 - (512 >> level) + (device >> level)
        pick = []
        for f in range(FAR):
            q = pup[f, node] - (512 - (512 >> level))
            if level == 0:
                tile, block = upper[q >> 3, (q >> 2) & 1], q & 3
            elif level == 1:
                tile, block = upper[q >> 2, 2], q & 3
            elif level == 2:
                tile, block = upper[q >> 1, 3], q & 1
            elif level == 3:
                tile, block = upper[q, 3], 2
            else:
                tile, block = upper_s[(8 if level == 4 else 12) + (q >> 2)], q & 3
            pick.append(everywhere(tile.astype(F32), block).astype(BF))
        rows.append(picks_of(pick))
    rows += [jnp.zeros((16, 256), BF)] * 2
    tiles = diagonal(dot_nt(jnp.concatenate(rows, axis=0), jnp.concatenate([block_up[0], block_up[1]], axis=1).astype(BF)))
    edge_rows = [me, 8 + (me >> 1), 12 + (me >> 2), 16 + branch, 48 + (branch >> 1)]
    current = everywhere(tiles[1], 1)
    for level in range(4, -1, -1):
        matrix = edges_up[pl.ds(pl.multiple_of(edge_rows[level] * 32, 32), 32), :]
        step = dot_nt(current.astype(BF), jnp.concatenate([matrix] * 4, axis=0))
        current = everywhere(tiles[level // 4], level % 4) + step

    for copy in fetched[12:]:
        copy.wait()
    rows6 = first_row(6) * 32
    local_s[63] = coupled_s[63] + dot_nt(current.astype(BF), edges[rows6 : rows6 + 128, :])
    rows5 = first_row(5) * 32
    local_s[62] = coupled_s[62] + dot_nt(local_s[63].astype(BF), edges[rows5 : rows5 + 128, :])
    for level in range(LEVELS - 3, -1, -1):
        parent = first_row(level + 1) // 4
        child = first_row(level) // 4
        for t in range((LEAVES >> level) // 8):
            start = (first_row(level) + 8 * t) * 32
            wide = dot_nt(local_s[parent + t].astype(BF), edges[start : start + 256, :])
            local_s[child + 2 * t] = coupled_s[child + 2 * t] + wide[:, 0:128]
            local_s[child + 2 * t + 1] = coupled_s[child + 2 * t + 1] + wide[:, 128:256]

    sum_s[...] = jnp.zeros((512, 256), F32)

    def back(c, carry):
        tall, hots = [], []
        lows = []
        for k in range(4):
            lanes = pl.ds(pl.multiple_of((4 * c + k) * 256, 256), 256)
            far = dot(local_s[4 * c + k].astype(BF), leaf_blocks(basis[:, lanes]))
            parts = []
            for half in range(2):
                first = near_s[16 * c + 4 * k + 2 * half]
                second = near_s[16 * c + 4 * k + 2 * half + 1]
                parts += [first, second]
            tall.append((far + INV_FOUR_PI * jnp.concatenate(parts, axis=1)).astype(BF))
            index = order[:, lanes]
            lows.append(jnp.broadcast_to((index >> 8).astype(F32), (16, 256)).astype(BF))
            fine = jnp.broadcast_to((index & 255).astype(F32), (16, 256)).astype(BF)
            fine = jnp.concatenate([fine] * 16, axis=0)
            hots.append(jnp.where(row_id == fine, jnp.ones((), BF), jnp.zeros((), BF)))
        total = jnp.concatenate(tall, axis=1)
        part = jnp.concatenate(lows, axis=1)
        none = jnp.zeros((16, 1024), BF)
        rows = jnp.concatenate(
            [jnp.where(part == jnp.asarray(low, BF), total, none) for low in range(32)], axis=0
        )
        sum_s[...] += dot_nt(rows, jnp.concatenate(hots, axis=1))
        return carry

    row_id = iota((256, 256), 0).astype(F32).astype(BF)
    lax.fori_loop(0, 8, back, 0)
    for low in range(32):
        out[:, 256 * low : 256 * low + 256] = sum_s[16 * low : 16 * low + 16, :]


def local(table, target, source, count, xyz, pool, blocks, codes, upper, edges_up, cup, pup, edges, basis, order):
    inputs = (table, target, source, count, xyz, pool, blocks, codes, upper, edges_up, cup, pup, edges, basis, order)
    scalars = (1, 2, 3, 7, 11)
    return pl.pallas_call(
        local_kernel,
        out_shape=jax.ShapeDtypeStruct((NRHS, POINTS), F32),
        in_specs=[HBM] * 15,
        out_specs=VMEM,
        scratch_shapes=[
            (pltpu.SMEM if i in scalars else pltpu.VMEM)(value.shape, value.dtype) for i, value in enumerate(inputs)
        ]
        + [
            pltpu.VMEM((2 * LEAVES + 2 * HALO, 16, 128), BF),
            pltpu.VMEM((LEAVES, 64, 64), BF),
            pltpu.VMEM((GROUP * TILES, 4, 16, 128), BF),
            pltpu.VMEM((2, 256, 128), F32),
            pltpu.VMEM((14, 16, 128), BF),
            pltpu.VMEM((TILES, 16, 128), F32),
            pltpu.VMEM((TILES, 16, 128), F32),
            pltpu.VMEM((LEAVES + 1, 16, 64), F32),
            pltpu.VMEM((512, 256), F32),
            pltpu.SemaphoreType.DMA((15,)),
        ],
        compiler_params=pltpu.CompilerParams(vmem_limit_bytes=64 * 1024 * 1024),
        name="local",
    )(*inputs)


def body(
    right_sides,
    positions,
    point_order,
    leaf_basis,
    transfer,
    couple_local,
    partner_local,
    transfer_up,
    couple_up,
    partner_up,
    send_list,
    side_list,
    pair_target,
    pair_source,
    pair_count,
):
    order = point_order.reshape(1, POINTS)
    table, pool, upper, edges, edges_up, cup, blocks, codes = exchange(
        right_sides, positions, order, leaf_basis, transfer, transfer_up,
        couple_up.transpose(1, 0, 2), couple_local.transpose(1, 0, 2), partner_local.T, send_list[0], side_list[0],
    )
    return local(
        table, pair_target, pair_source, pair_count, positions, pool.reshape(GROUP * TILES, 16, 128), blocks, codes,
        upper, edges_up, cup, partner_up.T, edges, leaf_basis, order,
    )


def solution(mesh):
    placed = (
        P(None, ("branch", "row", "top")),
        P(None, ("branch", "row", "top")),
        P(("branch", "row", "top")),
        P(None, ("branch", "row", "top")),
        P(("branch", "row", "top"), None),
        P(("branch", "row", "top"), None, None),
        P(("branch", "row", "top"), None),
        P(),
        P("top", None, None),
        P(),
        P(("branch", "row", "top"), None, None),
        P(("branch", "row", "top"), None, None),
        P(("branch", "row", "top"), None),
        P(("branch", "row", "top"), None),
        P(("branch", "row", "top")),
    )
    return jax.shard_map(
        body,
        mesh=mesh,
        in_specs=placed,
        out_specs=P(None, ("branch", "row", "top")),
        check_vma=False,
    )
```

```python
import jax
import jax.numpy as jnp
from jax import lax
from jax.experimental import pallas as pl
from jax.experimental.pallas import tpu as pltpu
from jax.sharding import PartitionSpec as P

LEAF = 64
RANK = 32
NRHS = 16
FAR = 6
SLOT = 16
HALO = 32
LEAVES = 128
POINTS = LEAVES * LEAF
NODES = 2 * LEAVES - 2
GROUP = 8
BRANCHES = 32
UPPER = 504
LEVELS = 7
TILES = 64
PITCH = 33
RECEIVED = GROUP * SLOT + 2 * HALO
OWN = 832

INV_FOUR_PI = 0.07957747154594767
SOFTENING = 0.01

BF = jnp.bfloat16
F32 = jnp.float32
I32 = jnp.int32
MESH = pl.DeviceIdType.MESH
VMEM = pl.BlockSpec(memory_space=pltpu.VMEM)
SMEM = pl.BlockSpec(memory_space=pltpu.SMEM)
HBM = pl.BlockSpec(memory_space=pltpu.HBM)


def dot(a, b):
    return jnp.dot(a, b, preferred_element_type=F32)


def dot_nt(a, b):
    return lax.dot_general(a, b, (((1,), (1,)), ((), ())), preferred_element_type=F32)


def iota(shape, axis):
    return lax.broadcasted_iota(I32, shape, axis)


def first_row(level):
    return 2 * LEAVES - 2 * (LEAVES >> level)


def block_turns(value):
    return [value] + [pltpu.roll(value, 32 * step, 1) for step in range(1, 4)]


def spread_edges(rows_of, put):
    value = rows_of(0)
    shape = value.shape
    owner = (iota(shape, 0) >> 1) & 3
    lane = iota(shape, 1) >> 5
    masks = [(owner == k) & (lane == k) for k in range(4)]
    for g in range(8):
        turns = block_turns(rows_of(g))
        for p in range(4):
            out = jnp.zeros(shape, F32)
            for k in range(4):
                out = jnp.where(masks[k], turns[(k - p) % 4], out)
            put(4 * g + p, out)


def spread_blocks(rows_of, put):
    lane = None
    for g in range(8):
        turns = [block_turns(rows_of(f, g)) for f in range(FAR)]
        if lane is None:
            lane = iota(turns[0][0].shape, 1) >> 5
        for a in range(4):
            pick = [turns[f][(f % 4 - a) % 4] for f in range(FAR)]
            low = jnp.where(
                lane == 0, pick[0], jnp.where(lane == 1, pick[1], jnp.where(lane == 2, pick[2], pick[3]))
            )
            high = jnp.where(lane == 0, pick[4], jnp.where(lane == 1, pick[5], 0.0))
            put(4 * g + a, low, high)


def stack_rows(rows, shape):
    sub = iota(shape, 0)
    out = jnp.zeros(shape, F32)
    for k, row in enumerate(rows):
        out = jnp.where(sub == k, row, out)
    return out


def split_three(value):
    high = value.astype(BF).astype(F32)
    rest = value - high
    middle = rest.astype(BF).astype(F32)
    return high, middle, rest - middle


def source_features(xyz):
    x, y, z = xyz[0:1], xyz[1:2], xyz[2:3]
    high, middle, low = split_three(x * x + y * y + z * z)
    return stack_rows([x, y, z, 1.0, 1.0, 1.0, high, middle, low], (16, xyz.shape[1]))


def target_features(xyz):
    x, y, z = xyz[0:1], xyz[1:2], xyz[2:3]
    high, middle, low = split_three(x * x + y * y + z * z + SOFTENING)
    return stack_rows(
        [-2.0 * x, -2.0 * y, -2.0 * z, high, middle, low, 1.0, 1.0, 1.0], (16, xyz.shape[1])
    )


def leaf_blocks(basis):
    lane = iota(basis.shape, 1) >> 6
    zero = jnp.zeros(basis.shape, basis.dtype)
    return jnp.concatenate([jnp.where(lane == j, basis, zero) for j in range(4)], axis=0)


def near_quad(goals, table, swapped, at, to, left):
    zero = jnp.zeros((16, 128), BF)
    lane16 = iota((64, 64), 1) >> 4
    g = [goals[to[i]] for i in range(4)]
    lhs = jnp.where(lane16 == 0, g[0], jnp.where(lane16 == 1, g[1], jnp.where(lane16 == 2, g[2], g[3])))
    value, other = [], []
    for i in range(4):
        plain, turned = table[at[i]], swapped[at[i]]
        if i % 2 == 0:
            pieces = [jnp.where(left, plain, zero), jnp.where(left, turned, zero)]
        else:
            pieces = [jnp.where(left, zero, turned), jnp.where(left, zero, plain)]
        for rows, piece in zip((value, other), pieces):
            rows.append(jnp.concatenate([piece, zero] if i < 2 else [zero, piece], axis=1))
    tile = lax.rsqrt(dot(lhs, jnp.concatenate(other, axis=0))).astype(BF)
    wide = dot_nt(jnp.concatenate(value, axis=0), tile)
    return [wide[16 * i : 16 * i + 16] for i in range(4)]


def swap_halves(table, swapped, count):
    def swap(c, carry):
        tiles = table[pl.ds(8 * c, 8)].reshape(128, 128).astype(F32)
        swapped[pl.ds(8 * c, 8)] = pltpu.roll(tiles, 64, 1).astype(BF).reshape(8, 16, 128)
        return carry

    lax.fori_loop(0, count // 8, swap, 0, unroll=4)


def exchange_kernel(
    rhs_h, xyz_h, order_h, basis_h, trans_h, tup_h, cup_h, couple_h, partner_h, send_h, side_h,
    target_h, source_h,
    table_o, pool_o, upper_o, edges_o, edges_up_o, cup_o, blocks_o, codes_o, goals_o, terms_o,
    rhs, xyz, order, basis, trans, tup, cup, couple, partner, send_s, side_s, target, source,
    x_s, table_s, pool_s, edge_s, tail_s, near_s, side_buf, root_s, roots_s, upper_s, cup_own, cup_send, cup_recv,
    edges, edges_up, block_s, block_tail, blocks, codes, goals_s, swap_s, terms,
    in_sem, near_send, near_recv, core_send, core_recv, ring_send, ring_recv,
    root_send, root_recv, up_send, up_recv, cup_sem, local_sem,
):
    branch = lax.axis_index("branch")
    row = lax.axis_index("row")
    top = lax.axis_index("top")
    me = row * 2 + top
    device = branch * GROUP + me

    held = (rhs, xyz, order, basis, trans, tup, cup, couple, partner, send_s, side_s, target, source)
    given = (rhs_h, xyz_h, order_h, basis_h, trans_h, tup_h, cup_h, couple_h, partner_h, send_h, side_h,
             target_h, source_h)
    fetched = [pltpu.make_async_copy(a, b, in_sem.at[i]) for i, (a, b) in enumerate(zip(given, held))]
    for i in (4, 0, 2, 1, 3, 9, 10, 5, 6, 8, 7, 11, 12):
        fetched[i].start()

    def member(index):
        return (branch, index // 2, index % 2)

    def peer(offset):
        return (me + offset) % GROUP

    def cousin(offset):
        return ((branch + offset) % BRANCHES, row, top)

    barrier = pltpu.get_barrier_semaphore()
    for offset in range(1, GROUP):
        pl.semaphore_signal(barrier, inc=1, device_id=member(peer(offset)), device_id_type=MESH)

    def greet(offset, carry):
        pl.semaphore_signal(barrier, inc=1, device_id=cousin(offset), device_id_type=MESH)
        return carry

    lax.fori_loop(1, BRANCHES, greet, 0)

    fetched[4].wait()
    tail_s[...] = jnp.zeros((16, 1024), F32)
    tail_s[0:14, :] = trans[240:254, :].astype(F32)

    def spread_one(rows_of, start, part):
        def put(p, out):
            edge_s[part, pl.ds(p, 16, stride=PITCH), :] = out

        spread_edges(rows_of, put)
        for u in range(16):
            rows = pl.ds(pl.multiple_of(start + 32 * u, 32), 32)
            edges[rows, :] = edge_s[part, PITCH * u : PITCH * u + 32].astype(BF)

    def spread(c, carry):
        for part in range(3):
            start = pl.multiple_of(48 * c + 16 * part, 16)
            spread_one(
                lambda g: trans[pl.ds(start, 16), 128 * g : 128 * g + 128].astype(F32),
                1536 * c + 512 * part, part,
            )
        return carry

    lax.fori_loop(0, 5, spread, 0)
    spread_one(lambda g: tail_s[:, 128 * g : 128 * g + 128], 7680, 0)

    for i in range(4):
        fetched[i].wait()
    for low in range(32):
        x_s[16 * low : 16 * low + 16, :] = rhs[:, 256 * low : 256 * low + 256]
    row_id = iota((256, 256), 0).astype(F32).astype(BF)
    left = iota((16, 128), 1) < 64

    def chunk(c, carry):
        lanes = pl.ds(pl.multiple_of(c * 512, 512), 512)
        index = order[:, lanes]
        fine = jnp.broadcast_to((index & 255).astype(F32), (16, 512)).astype(BF)
        hots = []
        for k in range(2):
            column = jnp.concatenate([fine[:, 256 * k : 256 * k + 256]] * 16, axis=0)
            hots.append(jnp.where(row_id == column, jnp.ones((), BF), jnp.zeros((), BF)))
        wide = dot(x_s[...], jnp.concatenate(hots, axis=1))
        part = jnp.broadcast_to(index >> 8, (16, 512))
        ordered = jnp.zeros((16, 512), F32)
        for low in range(32):
            ordered = jnp.where(part == low, wide[16 * low : 16 * low + 16], ordered)
        features = source_features(xyz[:, lanes].astype(F32))
        for half in range(4):
            value = ordered[:, 128 * half : 128 * half + 128]
            extra = features[:, 128 * half : 128 * half + 128]
            table_s[8 * c + 2 * half] = jnp.where(left, value, pltpu.roll(extra, 64, 1)).astype(BF)
            table_s[8 * c + 2 * half + 1] = jnp.where(left, pltpu.roll(value, 64, 1), extra).astype(BF)
        rounded = ordered.astype(BF)
        columns = basis[:, lanes]
        for k in range(2):
            pool_s[2 * c + k] = dot_nt(
                rounded[:, 256 * k : 256 * k + 256], leaf_blocks(columns[:, 256 * k : 256 * k + 256])
            ).astype(BF)
        return carry

    lax.fori_loop(0, 8, chunk, 0, unroll=2)
    pl.semaphore_wait(barrier, GROUP - 1 + BRANCHES - 1)

    sent = []

    def send(src, dst, send_sem, recv_sem, device_id):
        copy = pltpu.make_async_remote_copy(
            src_ref=src, dst_ref=dst, send_sem=send_sem, recv_sem=recv_sem,
            device_id=device_id, device_id_type=MESH,
        )
        copy.start()
        sent.append(copy)
        return copy

    kept = []

    def keep(src, dst, sem):
        copy = pltpu.make_async_copy(src, dst, sem)
        copy.start()
        kept.append(copy)

    partner_core = (branch, row, 1 - top)
    next_row = (branch, (row + 1) % 4, top)
    last_row = (branch, (row + 3) % 4, top)
    before = ((row + 3) % 4) * 2 + top
    after = ((row + 1) % 4) * 2 + top
    across = ((row + 2) % 4) * 2 + top

    parts = ((0, 16), (16, 16), (32, 32))

    def ring_first(p):
        tiles = pl.ds(*parts[p])
        src = pool_s.at[tiles]
        one = send(src, pool_o.at[me, tiles], ring_send.at[4 * p], ring_recv.at[4 * p], next_row)
        two = send(src, pool_o.at[me, tiles], ring_send.at[4 * p + 1], ring_recv.at[4 * p + 1], last_row)
        core = send(src, pool_o.at[me, tiles], core_send.at[5 * p], core_recv.at[5 * p], partner_core)
        return one, two, core

    def ring_second(p, first):
        tiles = pl.ds(*parts[p])
        first[0].wait_recv()
        lower = pl.ds(parts[p][0], parts[p][1] // 2)
        three = send(
            pool_o.at[before, lower], pool_o.at[before, lower],
            ring_send.at[4 * p + 2], ring_recv.at[4 * p + 2], next_row,
        )
        a = send(
            pool_o.at[before, tiles], pool_o.at[before, tiles],
            core_send.at[5 * p + 1], core_recv.at[5 * p + 1], partner_core,
        )
        first[1].wait_recv()
        higher = pl.ds(parts[p][0] + parts[p][1] // 2, parts[p][1] // 2)
        four = send(
            pool_o.at[after, higher], pool_o.at[after, higher],
            ring_send.at[4 * p + 3], ring_recv.at[4 * p + 3], last_row,
        )
        b = send(
            pool_o.at[after, tiles], pool_o.at[after, tiles],
            core_send.at[5 * p + 2], core_recv.at[5 * p + 2], partner_core,
        )
        return three, four, a, b

    def ring_third(p, second):
        second[0].wait_recv()
        lower = pl.ds(parts[p][0], parts[p][1] // 2)
        a = send(
            pool_o.at[across, lower], pool_o.at[across, lower],
            core_send.at[5 * p + 3], core_recv.at[5 * p + 3], partner_core,
        )
        second[1].wait_recv()
        higher = pl.ds(parts[p][0] + parts[p][1] // 2, parts[p][1] // 2)
        b = send(
            pool_o.at[across, higher], pool_o.at[across, higher],
            core_send.at[5 * p + 4], core_recv.at[5 * p + 4], partner_core,
        )
        return a, b

    first = [ring_first(0)]
    lax.fori_loop(8, 16, chunk, 0, unroll=2)
    first.append(ring_first(1))

    tile_of = [first_row(level) // 4 for level in range(LEVELS)]
    for level in range(LEVELS - 2):
        for t in range((LEAVES >> level) // 8):
            child = tile_of[level] + 2 * t
            pair = jnp.concatenate([pool_s[child], pool_s[child + 1]], axis=1)
            rows = (first_row(level) + 8 * t) * 32
            pool_s[tile_of[level + 1] + t] = dot(pair, edges[rows : rows + 256, :]).astype(BF)
    rows = first_row(5) * 32
    pool_s[63] = dot(pool_s[62], edges[rows : rows + 128, :]).astype(BF)
    rows = first_row(6) * 32
    root = dot(pool_s[63], edges[rows : rows + 128, :])
    placed = root
    for k in (0, 1, 3):
        placed = jnp.where(me % 4 == k, pltpu.roll(root, (32 * (k - 2)) % 128, 1), placed)
    root_s[...] = placed.astype(BF)
    roots = []
    for offset in range(1, GROUP):
        roots.append(
            send(
                root_s, roots_s.at[me],
                root_send.at[offset - 1], root_recv.at[offset - 1], member(peer(offset)),
            )
        )
    roots_s[me] = root_s[...]
    arriving = [first[0][2], first[1][2]]
    fetched[9].wait()
    fetched[10].wait()

    def fill(k, carry):
        for m in range(GROUP):
            near_s[m, k] = table_s[send_s[m, k]]
        for s in range(2):
            side_buf[s, 2 * k] = table_s[side_s[s, 2 * k]]
            side_buf[s, 2 * k + 1] = table_s[side_s[s, 2 * k + 1]]
        return carry

    lax.fori_loop(0, SLOT, fill, 0)

    for offset in range(1, GROUP):
        arriving.append(
            send(
                near_s.at[peer(offset)], table_o.at[pl.ds(me * SLOT, SLOT)],
                near_send.at[offset - 1], near_recv.at[offset - 1], member(peer(offset)),
            )
        )
    arriving.append(
        send(
            side_buf.at[1], table_o.at[pl.ds(LEAVES, HALO)],
            near_send.at[7], near_recv.at[7], cousin(1),
        )
    )
    arriving.append(
        send(
            side_buf.at[0], table_o.at[pl.ds(LEAVES + HALO, HALO)],
            near_send.at[8], near_recv.at[8], cousin(BRANCHES - 1),
        )
    )
    keep(near_s.at[me], table_o.at[pl.ds(me * SLOT, SLOT)], local_sem.at[1])

    first.append(ring_first(2))
    arriving.append(first[2][2])
    keep(pool_s, pool_o.at[me], local_sem.at[2])
    keep(edges, edges_o, local_sem.at[4])

    fetched[5].wait()
    slot = iota((64, 496), 0)
    want = jnp.where(
        slot < 8,
        8 * branch + slot,
        jnp.where(
            slot < 12,
            248 + 4 * branch + slot,
            jnp.where(slot < 14, 372 + 2 * branch + slot, jnp.where(slot < 16, -1, 432 + slot)),
        ),
    )
    chosen = dot((iota((64, 496), 1) == want).astype(F32).astype(BF), tup[...])

    def put_up(p, out):
        edge_s[0, pl.ds(p, 64, stride=PITCH), :] = out

    spread_edges(lambda g: chosen[:, 128 * g : 128 * g + 128], put_up)
    for u in range(64):
        edges_up[32 * u : 32 * u + 32, :] = edge_s[0, PITCH * u : PITCH * u + 32].astype(BF)
    keep(edges_up, edges_up_o, local_sem.at[5])

    for copy in roots:
        copy.wait_recv()
    low = roots_s[0] + roots_s[1] + roots_s[2] + roots_s[3]
    high = roots_s[4] + roots_s[5] + roots_s[6] + roots_s[7]
    upper_s[0] = low
    upper_s[1] = high
    level1 = dot(jnp.concatenate([low, high], axis=1), edges_up[0:256, :]).astype(BF)
    upper_s[2] = level1
    level2 = dot(level1, edges_up[256:384, :]).astype(BF)
    level3 = dot(level2[:, 0:64], edges_up[384:448, :]).astype(BF)
    upper_s[3] = jnp.where(left, level2.astype(F32), level3.astype(F32)).astype(BF)

    def spread_up(offset, carry):
        pltpu.make_async_remote_copy(
            src_ref=upper_s, dst_ref=upper_o.at[branch],
            send_sem=up_send.at[offset - 1], recv_sem=up_recv.at[offset - 1],
            device_id=cousin(offset), device_id_type=MESH,
        ).start()
        return carry

    lax.fori_loop(1, BRANCHES, spread_up, 0)
    keep(upper_s, upper_o.at[branch], local_sem.at[3])

    fetched[6].wait()
    slot = iota((16, 252), 0)
    shape = slot & 7
    base = jnp.where(slot < 8, device, device + 1 - 2 * top)
    node = jnp.full((16, 252), -1, I32)
    for level in range(6):
        node = jnp.where(shape == level, 512 - (512 >> level) + (base >> level), node)
    hot = (iota((16, 252), 1) + 252 * top == node).astype(F32).astype(BF)
    for f in range(FAR):
        chosen = dot(hot, cup[f])
        cup_own[f] = chosen[0:8]
        cup_send[f] = chosen[8:16]
    cup_copy = send(cup_send, cup_recv, cup_sem.at[0], cup_sem.at[1], partner_core)

    fetched[8].wait()
    column = iota((FAR, 254), 1)
    width = jnp.full((FAR, 254), 7, I32)
    start = jnp.zeros((FAR, 254), I32)
    for level in range(1, LEVELS):
        width = jnp.where(column >= first_row(level), 7 - level, width)
        start = jnp.where(column >= first_row(level), first_row(level), start)
    codes[:, 254:256] = jnp.zeros((FAR, 2), I32)
    codes[:, 0:254] = (partner[...] >> width) * 256 + start + (partner[...] & ((1 << width) - 1))
    keep(codes, codes_o, local_sem.at[6])

    second = [ring_second(0, first[0]), ring_second(1, first[1])]
    arriving += second[0][2:] + second[1][2:]

    fetched[7].wait()
    for f in range(FAR):
        block_tail[f] = jnp.zeros((16, 1024), F32)
        block_tail[f, 0:14, :] = couple[f, 240:254, :].astype(F32)

    def couple_one(rows_of, start, part):
        def put(a, low, high):
            block_s[part, 0, pl.ds(a, 16, stride=PITCH), :] = low
            block_s[part, 1, pl.ds(a, 16, stride=PITCH), :] = high

        spread_blocks(rows_of, put)
        for half in range(2):
            for u in range(16):
                rows = pl.ds(pl.multiple_of(start + 32 * u, 32), 32)
                blocks[rows, 128 * half : 128 * half + 128] = block_s[
                    part, half, PITCH * u : PITCH * u + 32
                ].astype(BF)

    def couple_rows(c, carry):
        start = pl.multiple_of(16 * c, 16)
        couple_one(
            lambda f, g: couple[f, pl.ds(start, 16), 128 * g : 128 * g + 128].astype(F32),
            512 * c, 0,
        )
        return carry

    lax.fori_loop(0, 15, couple_rows, 0)
    couple_one(lambda f, g: block_tail[f, :, 128 * g : 128 * g + 128], 7680, 0)
    keep(blocks, blocks_o, local_sem.at[7])
    second.append(ring_second(2, first[2]))
    arriving += second[2][2:]

    eye = (iota((128, 128), 0) == iota((128, 128), 1)).astype(F32).astype(BF)

    def goals(c, carry):
        lanes = pl.ds(pl.multiple_of(c * 128, 128), 128)
        features = target_features(xyz[:, lanes].astype(F32)).astype(BF)
        turned = dot_nt(eye, jnp.concatenate([features] * 4, axis=0)).astype(BF)
        goals_s[2 * c] = turned[0:64]
        goals_s[2 * c + 1] = turned[64:128]
        return carry

    lax.fori_loop(0, 64, goals, 0, unroll=16)
    keep(goals_s, goals_o, local_sem.at[9])
    swap_halves(table_s, swap_s, LEAVES)
    fetched[11].wait()
    fetched[12].wait()

    def own_pairs(c, carry):
        for k in range(16):
            place = 64 * c + 4 * k
            at = [jnp.minimum(source[0, RECEIVED + place + i], LEAVES - 1) for i in range(4)]
            to = [target[0, RECEIVED + place + i] for i in range(4)]
            for i, part in enumerate(near_quad(goals_s, table_s, swap_s, at, to, left)):
                terms[place + i] = part.astype(BF)
        return carry

    for k, (start, stop) in enumerate(((0, 5), (5, 9), (9, 13))):
        lax.fori_loop(start, stop, own_pairs, 0)
        span = pl.ds(64 * start, 64 * (stop - start))
        keep(terms.at[span], terms_o.at[span], local_sem.at[10 + k])
        arriving += ring_third(k, second[k])

    cup_copy.wait_recv()
    cup_own[...] = cup_own[...] + cup_recv[...]
    keep(cup_own, cup_o, local_sem.at[8])
    for copy in arriving:
        copy.wait_recv()
    for copy in sent:
        copy.wait_send()

    def finish(offset, carry):
        pltpu.make_async_remote_copy(
            src_ref=upper_s, dst_ref=upper_o.at[branch],
            send_sem=up_send.at[offset - 1], recv_sem=up_recv.at[offset - 1],
            device_id=cousin(offset), device_id_type=MESH,
        ).wait()
        return carry

    lax.fori_loop(1, BRANCHES, finish, 0)
    for copy in kept:
        copy.wait()


def exchange(rhs, xyz, order, basis, trans, tup, cup, couple, partner, send_list, side_list, target, source):
    shape = jax.ShapeDtypeStruct
    inputs = (rhs, xyz, order, basis, trans, tup, cup, couple, partner, send_list, side_list, target, source)
    return pl.pallas_call(
        exchange_kernel,
        out_shape=(
            shape((RECEIVED, 16, 128), BF),
            shape((GROUP, TILES, 16, 128), BF),
            shape((BRANCHES, 4, 16, 128), BF),
            shape((8192, 128), BF),
            shape((2048, 128), BF),
            shape((FAR, 8, 1024), F32),
            shape((8192, 256), BF),
            shape((FAR, 256), I32),
            shape((LEAVES, 64, 64), BF),
            shape((OWN, 16, 64), BF),
        ),
        in_specs=[HBM] * 13,
        out_specs=(HBM,) * 10,
        scratch_shapes=[pltpu.VMEM(value.shape, value.dtype) for value in inputs[:9]]
        + [pltpu.SMEM(value.shape, value.dtype) for value in inputs[9:]]
        + [
            pltpu.VMEM((512, 256), BF),
            pltpu.VMEM((LEAVES, 16, 128), BF),
            pltpu.VMEM((TILES, 16, 128), BF),
            pltpu.VMEM((3, 64 * PITCH, 128), F32),
            pltpu.VMEM((16, 1024), F32),
            pltpu.VMEM((GROUP, SLOT, 16, 128), BF),
            pltpu.VMEM((2, HALO, 16, 128), BF),
            pltpu.VMEM((16, 128), BF),
            pltpu.VMEM((GROUP, 16, 128), BF),
            pltpu.VMEM((4, 16, 128), BF),
            pltpu.VMEM((FAR, 8, 1024), F32),
            pltpu.VMEM((FAR, 8, 1024), F32),
            pltpu.VMEM((FAR, 8, 1024), F32),
            pltpu.VMEM((8192, 128), BF),
            pltpu.VMEM((2048, 128), BF),
            pltpu.VMEM((1, 2, 16 * PITCH, 128), F32),
            pltpu.VMEM((FAR, 16, 1024), F32),
            pltpu.VMEM((8192, 256), BF),
            pltpu.VMEM((FAR, 256), I32),
            pltpu.VMEM((LEAVES, 64, 64), BF),
            pltpu.VMEM((LEAVES, 16, 128), BF),
            pltpu.VMEM((OWN, 16, 64), BF),
        ]
        + [
            pltpu.SemaphoreType.DMA((count,))
            for count in (13, 9, 9, 15, 15, 12, 12, 7, 7, BRANCHES - 1, BRANCHES - 1, 2, 13)
        ],
        compiler_params=pltpu.CompilerParams(
            collective_id=0, has_side_effects=True, vmem_limit_bytes=64 * 1024 * 1024
        ),
        name="exchange",
    )(*inputs)


def local_kernel(
    table_h, target_h, source_h, count_h, goals_h, terms_h, pool_h, blocks_h, codes_h, upper_h, edges_up_h, cup_h, pup_h,
    edges_h, basis_h, order_h,
    out,
    table, target, source, count, goals, terms, pool, blocks, codes, upper, edges_up, cup, pup, edges, basis, order,
    swap_s, pool_rep, block_up, upper_s, coupled_s, local_s, near_s, sum_s, in_sem,
):
    given = (table_h, target_h, source_h, count_h, goals_h, terms_h, pool_h, blocks_h, codes_h, upper_h, edges_up_h, cup_h, pup_h,
             edges_h, basis_h, order_h)
    held = (table, target, source, count, goals, terms, pool, blocks, codes, upper, edges_up, cup, pup, edges, basis, order)
    fetched = [pltpu.make_async_copy(a, b, in_sem.at[i]) for i, (a, b) in enumerate(zip(given, held))]
    for copy in fetched:
        copy.start()
    branch = lax.axis_index("branch")
    me = lax.axis_index("row") * 2 + lax.axis_index("top")
    device = branch * GROUP + me
    left = iota((16, 128), 1) < 64
    lane_block = iota((16, 128), 1) >> 5

    def clear(t, carry):
        near_s[t] = jnp.zeros((16, 64), F32)
        return carry

    lax.fori_loop(0, LEAVES + 1, clear, 0, unroll=3)

    for copy in fetched[:5]:
        copy.wait()
    swap_halves(table, swap_s, RECEIVED)
    zero = jnp.zeros((16, 128), BF)

    def near(c, carry):
        outs = []
        for k in range(16):
            place = 64 * c + 4 * k
            at = [source[0, place + i] - LEAVES for i in range(4)]
            to = [target[0, place + i] for i in range(4)]
            outs += zip(to, near_quad(goals, table, swap_s, at, to, left))
        for goal, part in outs:
            near_s[goal] = near_s[goal] + part
        return carry

    lax.fori_loop(0, RECEIVED // 64, near, 0)
    fetched[5].wait()
    live = count[0] - RECEIVED

    def add_terms(c, carry):
        for k in range(16):
            place = 16 * c + k
            goal = jnp.where(place < live, target[0, RECEIVED + place], LEAVES)
            near_s[goal] = near_s[goal] + terms[place].astype(F32)
        return carry

    lax.fori_loop(0, (live + 15) // 16, add_terms, 0)

    for copy in fetched[6:13]:
        copy.wait()

    def put_up(a, low, high):
        block_up[0, pl.ds(a, 8, stride=32), :] = low
        block_up[1, pl.ds(a, 8, stride=32), :] = high

    spread_blocks(lambda f, g: cup[f, :, 128 * g : 128 * g + 128], put_up)

    wide_block = iota((128, 128), 1) >> 5

    def widen(t, carry):
        tiles = pool[pl.ds(8 * t, 8)].reshape(128, 128).astype(F32)
        turns = [v.astype(BF) for v in block_turns(tiles)]
        for j in range(4):
            value = turns[(3 - j) % 4]
            for k in range(3):
                value = jnp.where(wide_block == k, turns[(k - j) % 4], value)
            pool_rep[pl.ds(8 * t, 8), j] = value.reshape(8, 16, 128)
        return carry

    lax.fori_loop(0, GROUP * TILES // 8, widen, 0, unroll=4)

    def picks_of(pick):
        low = jnp.where(
            lane_block == 0,
            pick[0],
            jnp.where(lane_block == 1, pick[1], jnp.where(lane_block == 2, pick[2], pick[3])),
        )
        high = jnp.where(lane_block == 0, pick[4], jnp.where(lane_block == 1, pick[5], zero))
        return jnp.concatenate([low, high], axis=1)

    def diagonal(wide):
        tiles = []
        for half in range(2):
            tile = wide[64 * half + 48 : 64 * half + 64, 128 * half : 128 * half + 128]
            for j in range(3):
                start = 64 * half + 16 * j
                tile = jnp.where(
                    lane_block == j, wide[start : start + 16, 128 * half : 128 * half + 128], tile
                )
            tiles.append(tile)
        return tiles

    def coupling(c, carry):
        rows = []
        for u in range(8):
            rows.append(picks_of([pool_rep[codes[f, 8 * c + u] >> 2, codes[f, 8 * c + u] & 3] for f in range(FAR)]))
        matrices = blocks[pl.ds(pl.multiple_of(c * 256, 256), 256), :]
        tiles = diagonal(dot_nt(jnp.concatenate(rows, axis=0), matrices))
        coupled_s[2 * c] = tiles[0]
        coupled_s[2 * c + 1] = tiles[1]
        return carry

    lax.fori_loop(0, 32, coupling, 0, unroll=4)

    def thirds(t, carry):
        tile = jnp.zeros((16, 128), F32)
        for j in range(4):
            tile = jnp.where(
                lane_block == j, pltpu.roll(upper[4 * t + j, 3].astype(F32), (32 * (j - 2)) % 128, 1), tile
            )
        upper_s[t] = tile.astype(BF)
        return carry

    lax.fori_loop(0, 8, thirds, 0)
    for t in range(4):
        pair = jnp.concatenate([upper_s[2 * t], upper_s[2 * t + 1]], axis=1)
        upper_s[8 + t] = dot(pair, edges_up[512 + 256 * t : 768 + 256 * t, :]).astype(BF)
    for t in range(2):
        pair = jnp.concatenate([upper_s[8 + 2 * t], upper_s[9 + 2 * t]], axis=1)
        upper_s[12 + t] = dot(pair, edges_up[1536 + 256 * t : 1792 + 256 * t, :]).astype(BF)

    def everywhere(tile, block):
        only = jnp.where(lane_block == block, tile, 0.0)
        only = only + pltpu.roll(only, 32, 1)
        return only + pltpu.roll(only, 64, 1)

    rows = []
    for level in range(6):
        node = 512 - (512 >> level) + (device >> level)
        pick = []
        for f in range(FAR):
            q = pup[f, node] - (512 - (512 >> level))
            if level == 0:
                tile, block = upper[q >> 3, (q >> 2) & 1], q & 3
            elif level == 1:
                tile, block = upper[q >> 2, 2], q & 3
            elif level == 2:
                tile, block = upper[q >> 1, 3], q & 1
            elif level == 3:
                tile, block = upper[q, 3], 2
            else:
                tile, block = upper_s[(8 if level == 4 else 12) + (q >> 2)], q & 3
            pick.append(everywhere(tile.astype(F32), block).astype(BF))
        rows.append(picks_of(pick))
    rows += [jnp.zeros((16, 256), BF)] * 2
    tiles = diagonal(dot_nt(jnp.concatenate(rows, axis=0), jnp.concatenate([block_up[0], block_up[1]], axis=1).astype(BF)))
    edge_rows = [me, 8 + (me >> 1), 12 + (me >> 2), 16 + branch, 48 + (branch >> 1)]
    current = everywhere(tiles[1], 1)
    for level in range(4, -1, -1):
        matrix = edges_up[pl.ds(pl.multiple_of(edge_rows[level] * 32, 32), 32), :]
        step = dot_nt(current.astype(BF), jnp.concatenate([matrix] * 4, axis=0))
        current = everywhere(tiles[level // 4], level % 4) + step

    for copy in fetched[13:]:
        copy.wait()
    rows6 = first_row(6) * 32
    local_s[63] = coupled_s[63] + dot_nt(current.astype(BF), edges[rows6 : rows6 + 128, :])
    rows5 = first_row(5) * 32
    local_s[62] = coupled_s[62] + dot_nt(local_s[63].astype(BF), edges[rows5 : rows5 + 128, :])
    for level in range(LEVELS - 3, -1, -1):
        parent = first_row(level + 1) // 4
        child = first_row(level) // 4
        for t in range((LEAVES >> level) // 8):
            start = (first_row(level) + 8 * t) * 32
            wide = dot_nt(local_s[parent + t].astype(BF), edges[start : start + 256, :])
            local_s[child + 2 * t] = coupled_s[child + 2 * t] + wide[:, 0:128]
            local_s[child + 2 * t + 1] = coupled_s[child + 2 * t + 1] + wide[:, 128:256]

    sum_s[...] = jnp.zeros((512, 256), F32)

    def back(c, carry):
        tall, hots = [], []
        lows = []
        for k in range(4):
            lanes = pl.ds(pl.multiple_of((4 * c + k) * 256, 256), 256)
            far = dot(local_s[4 * c + k].astype(BF), leaf_blocks(basis[:, lanes]))
            parts = []
            for half in range(2):
                first = near_s[16 * c + 4 * k + 2 * half]
                second = near_s[16 * c + 4 * k + 2 * half + 1]
                parts += [first, second]
            tall.append((far + INV_FOUR_PI * jnp.concatenate(parts, axis=1)).astype(BF))
            index = order[:, lanes]
            lows.append(jnp.broadcast_to((index >> 8).astype(F32), (16, 256)).astype(BF))
            fine = jnp.broadcast_to((index & 255).astype(F32), (16, 256)).astype(BF)
            fine = jnp.concatenate([fine] * 16, axis=0)
            hots.append(jnp.where(row_id == fine, jnp.ones((), BF), jnp.zeros((), BF)))
        total = jnp.concatenate(tall, axis=1)
        part = jnp.concatenate(lows, axis=1)
        none = jnp.zeros((16, 1024), BF)
        rows = jnp.concatenate(
            [jnp.where(part == jnp.asarray(low, BF), total, none) for low in range(32)], axis=0
        )
        sum_s[...] += dot_nt(rows, jnp.concatenate(hots, axis=1))
        return carry

    row_id = iota((256, 256), 0).astype(F32).astype(BF)
    lax.fori_loop(0, 8, back, 0)
    for low in range(32):
        out[:, 256 * low : 256 * low + 256] = sum_s[16 * low : 16 * low + 16, :]


def local(*inputs):
    scalars = (1, 2, 3, 8, 12)
    return pl.pallas_call(
        local_kernel,
        out_shape=jax.ShapeDtypeStruct((NRHS, POINTS), F32),
        in_specs=[HBM] * 16,
        out_specs=VMEM,
        scratch_shapes=[
            (pltpu.SMEM if i in scalars else pltpu.VMEM)(value.shape, value.dtype) for i, value in enumerate(inputs)
        ]
        + [
            pltpu.VMEM((RECEIVED, 16, 128), BF),
            pltpu.VMEM((GROUP * TILES, 4, 16, 128), BF),
            pltpu.VMEM((2, 256, 128), F32),
            pltpu.VMEM((14, 16, 128), BF),
            pltpu.VMEM((TILES, 16, 128), F32),
            pltpu.VMEM((TILES, 16, 128), F32),
            pltpu.VMEM((LEAVES + 1, 16, 64), F32),
            pltpu.VMEM((512, 256), F32),
            pltpu.SemaphoreType.DMA((16,)),
        ],
        compiler_params=pltpu.CompilerParams(vmem_limit_bytes=64 * 1024 * 1024),
        name="local",
    )(*inputs)


def body(
    right_sides,
    positions,
    point_order,
    leaf_basis,
    transfer,
    couple_local,
    partner_local,
    transfer_up,
    couple_up,
    partner_up,
    send_list,
    side_list,
    pair_target,
    pair_source,
    pair_count,
):
    order = point_order.reshape(1, POINTS)
    table, pool, upper, edges, edges_up, cup, blocks, codes, goals, terms = exchange(
        right_sides, positions, order, leaf_basis, transfer, transfer_up,
        couple_up.transpose(1, 0, 2), couple_local.transpose(1, 0, 2), partner_local.T, send_list[0], side_list[0],
        pair_target, pair_source,
    )
    return local(
        table, pair_target, pair_source, pair_count, goals, terms, pool.reshape(GROUP * TILES, 16, 128), blocks, codes,
        upper, edges_up, cup, partner_up.T, edges, leaf_basis, order,
    )


def solution(mesh):
    placed = (
        P(None, ("branch", "row", "top")),
        P(None, ("branch", "row", "top")),
        P(("branch", "row", "top")),
        P(None, ("branch", "row", "top")),
        P(("branch", "row", "top"), None),
        P(("branch", "row", "top"), None, None),
        P(("branch", "row", "top"), None),
        P(),
        P("top", None, None),
        P(),
        P(("branch", "row", "top"), None, None),
        P(("branch", "row", "top"), None, None),
        P(("branch", "row", "top"), None),
        P(("branch", "row", "top"), None),
        P(("branch", "row", "top")),
    )
    return jax.shard_map(
        body,
        mesh=mesh,
        in_specs=placed,
        out_specs=P(None, ("branch", "row", "top")),
        check_vma=False,
    )
```

```python
import jax
import jax.numpy as jnp
from jax import lax
from jax.experimental import pallas as pl
from jax.experimental.pallas import tpu as pltpu
from jax.sharding import PartitionSpec as P

LEAF = 64
RANK = 32
NRHS = 16
FAR = 6
SLOT = 16
HALO = 32
LEAVES = 128
POINTS = LEAVES * LEAF
NODES = 2 * LEAVES - 2
GROUP = 8
BRANCHES = 32
UPPER = 504
LEVELS = 7
TILES = 64
PITCH = 33
RECEIVED = GROUP * SLOT + 2 * HALO
OWN = 832

INV_FOUR_PI = 0.07957747154594767
SOFTENING = 0.01

BF = jnp.bfloat16
F32 = jnp.float32
I32 = jnp.int32
MESH = pl.DeviceIdType.MESH
VMEM = pl.BlockSpec(memory_space=pltpu.VMEM)
SMEM = pl.BlockSpec(memory_space=pltpu.SMEM)
HBM = pl.BlockSpec(memory_space=pltpu.HBM)


def dot(a, b):
    return jnp.dot(a, b, preferred_element_type=F32)


def dot_nt(a, b):
    return lax.dot_general(a, b, (((1,), (1,)), ((), ())), preferred_element_type=F32)


def iota(shape, axis):
    return lax.broadcasted_iota(I32, shape, axis)


def first_row(level):
    return 2 * LEAVES - 2 * (LEAVES >> level)


def block_turns(value):
    return [value] + [pltpu.roll(value, 32 * step, 1) for step in range(1, 4)]


def spread_edges(rows_of, put):
    value = rows_of(0)
    shape = value.shape
    owner = (iota(shape, 0) >> 1) & 3
    lane = iota(shape, 1) >> 5
    masks = [(owner == k) & (lane == k) for k in range(4)]
    for g in range(8):
        turns = block_turns(rows_of(g))
        for p in range(4):
            out = jnp.zeros(shape, F32)
            for k in range(4):
                out = jnp.where(masks[k], turns[(k - p) % 4], out)
            put(4 * g + p, out)


def spread_blocks(rows_of, put):
    lane = None
    for g in range(8):
        turns = [block_turns(rows_of(f, g)) for f in range(FAR)]
        if lane is None:
            lane = iota(turns[0][0].shape, 1) >> 5
        for a in range(4):
            pick = [turns[f][(f % 4 - a) % 4] for f in range(FAR)]
            low = jnp.where(
                lane == 0, pick[0], jnp.where(lane == 1, pick[1], jnp.where(lane == 2, pick[2], pick[3]))
            )
            high = jnp.where(lane == 0, pick[4], jnp.where(lane == 1, pick[5], 0.0))
            put(4 * g + a, low, high)


def stack_rows(rows, shape):
    sub = iota(shape, 0)
    out = jnp.zeros(shape, F32)
    for k, row in enumerate(rows):
        out = jnp.where(sub == k, row, out)
    return out


def split_three(value):
    high = value.astype(BF).astype(F32)
    rest = value - high
    middle = rest.astype(BF).astype(F32)
    return high, middle, rest - middle


def source_features(xyz):
    x, y, z = xyz[0:1], xyz[1:2], xyz[2:3]
    high, middle, low = split_three(x * x + y * y + z * z)
    return stack_rows([x, y, z, 1.0, 1.0, 1.0, high, middle, low], (16, xyz.shape[1]))


def target_features(xyz):
    x, y, z = xyz[0:1], xyz[1:2], xyz[2:3]
    high, middle, low = split_three(x * x + y * y + z * z + SOFTENING)
    return stack_rows(
        [-2.0 * x, -2.0 * y, -2.0 * z, high, middle, low, 1.0, 1.0, 1.0], (16, xyz.shape[1])
    )


def leaf_blocks(basis):
    lane = iota(basis.shape, 1) >> 6
    zero = jnp.zeros(basis.shape, basis.dtype)
    return jnp.concatenate([jnp.where(lane == j, basis, zero) for j in range(4)], axis=0)


def near_quad(goals, table, swapped, at, to, left):
    zero = jnp.zeros((16, 128), BF)
    lane16 = iota((64, 64), 1) >> 4
    g = [goals[to[i]] for i in range(4)]
    lhs = jnp.where(lane16 == 0, g[0], jnp.where(lane16 == 1, g[1], jnp.where(lane16 == 2, g[2], g[3])))
    value, other = [], []
    for i in range(4):
        plain, turned = table[at[i]], swapped[at[i]]
        if i % 2 == 0:
            pieces = [jnp.where(left, plain, zero), jnp.where(left, turned, zero)]
        else:
            pieces = [jnp.where(left, zero, turned), jnp.where(left, zero, plain)]
        for rows, piece in zip((value, other), pieces):
            rows.append(jnp.concatenate([piece, zero] if i < 2 else [zero, piece], axis=1))
    tile = lax.rsqrt(dot(lhs, jnp.concatenate(other, axis=0))).astype(BF)
    wide = dot_nt(jnp.concatenate(value, axis=0), tile)
    return [wide[16 * i : 16 * i + 16] for i in range(4)]


def swap_halves(table, swapped, count):
    def swap(c, carry):
        tiles = table[pl.ds(8 * c, 8)].reshape(128, 128).astype(F32)
        swapped[pl.ds(8 * c, 8)] = pltpu.roll(tiles, 64, 1).astype(BF).reshape(8, 16, 128)
        return carry

    lax.fori_loop(0, count // 8, swap, 0, unroll=4)


def exchange_kernel(
    rhs_h, xyz_h, order_h, basis_h, trans_h, tup_h, cup_h, couple_h, partner_h, send_h, side_h,
    target_h, source_h,
    table_o, pool_o, upper_o, edges_o, edges_up_o, cup_o, blocks_o, codes_o, goals_o, terms_o,
    rhs, xyz, order, basis, trans, tup, cup, couple, partner, send_s, side_s, target, source,
    x_s, table_s, pool_s, edge_s, tail_s, near_s, side_buf, root_s, roots_s, upper_s, cup_own, cup_send, cup_recv,
    edges, edges_up, block_s, block_tail, blocks, codes, goals_s, swap_s, terms,
    in_sem, near_send, near_recv, core_send, core_recv, ring_send, ring_recv,
    root_send, root_recv, up_send, up_recv, cup_sem, local_sem,
):
    branch = lax.axis_index("branch")
    row = lax.axis_index("row")
    top = lax.axis_index("top")
    me = row * 2 + top
    device = branch * GROUP + me

    held = (rhs, xyz, order, basis, trans, tup, cup, couple, partner, send_s, side_s, target, source)
    given = (rhs_h, xyz_h, order_h, basis_h, trans_h, tup_h, cup_h, couple_h, partner_h, send_h, side_h,
             target_h, source_h)
    fetched = [pltpu.make_async_copy(a, b, in_sem.at[i]) for i, (a, b) in enumerate(zip(given, held))]
    for i in (4, 0, 2, 1, 3, 9, 10, 5, 6, 8, 7, 11, 12):
        fetched[i].start()

    def member(index):
        return (branch, index // 2, index % 2)

    def peer(offset):
        return (me + offset) % GROUP

    def cousin(offset):
        return ((branch + offset) % BRANCHES, row, top)

    barrier = pltpu.get_barrier_semaphore()
    for offset in range(1, GROUP):
        pl.semaphore_signal(barrier, inc=1, device_id=member(peer(offset)), device_id_type=MESH)

    def greet(offset, carry):
        pl.semaphore_signal(barrier, inc=1, device_id=cousin(offset), device_id_type=MESH)
        return carry

    lax.fori_loop(1, BRANCHES, greet, 0)

    fetched[4].wait()
    tail_s[...] = jnp.zeros((16, 1024), F32)
    tail_s[0:14, :] = trans[240:254, :].astype(F32)

    def spread_one(rows_of, start, part):
        def put(p, out):
            edge_s[part, pl.ds(p, 16, stride=PITCH), :] = out

        spread_edges(rows_of, put)
        for u in range(16):
            rows = pl.ds(pl.multiple_of(start + 32 * u, 32), 32)
            edges[rows, :] = edge_s[part, PITCH * u : PITCH * u + 32].astype(BF)

    def spread(c, carry):
        for part in range(3):
            start = pl.multiple_of(48 * c + 16 * part, 16)
            spread_one(
                lambda g: trans[pl.ds(start, 16), 128 * g : 128 * g + 128].astype(F32),
                1536 * c + 512 * part, part,
            )
        return carry

    lax.fori_loop(0, 5, spread, 0)
    spread_one(lambda g: tail_s[:, 128 * g : 128 * g + 128], 7680, 0)

    for i in range(4):
        fetched[i].wait()
    for low in range(32):
        x_s[16 * low : 16 * low + 16, :] = rhs[:, 256 * low : 256 * low + 256]
    row_id = iota((256, 256), 0).astype(F32).astype(BF)
    left = iota((16, 128), 1) < 64

    def chunk(c, carry):
        lanes = pl.ds(pl.multiple_of(c * 512, 512), 512)
        index = order[:, lanes]
        fine = jnp.broadcast_to((index & 255).astype(F32), (16, 512)).astype(BF)
        hots = []
        for k in range(2):
            column = jnp.concatenate([fine[:, 256 * k : 256 * k + 256]] * 16, axis=0)
            hots.append(jnp.where(row_id == column, jnp.ones((), BF), jnp.zeros((), BF)))
        wide = dot(x_s[...], jnp.concatenate(hots, axis=1))
        part = jnp.broadcast_to(index >> 8, (16, 512))
        ordered = jnp.zeros((16, 512), F32)
        for low in range(32):
            ordered = jnp.where(part == low, wide[16 * low : 16 * low + 16], ordered)
        features = source_features(xyz[:, lanes].astype(F32))
        for half in range(4):
            value = ordered[:, 128 * half : 128 * half + 128]
            extra = features[:, 128 * half : 128 * half + 128]
            table_s[8 * c + 2 * half] = jnp.where(left, value, pltpu.roll(extra, 64, 1)).astype(BF)
            table_s[8 * c + 2 * half + 1] = jnp.where(left, pltpu.roll(value, 64, 1), extra).astype(BF)
        rounded = ordered.astype(BF)
        columns = basis[:, lanes]
        for k in range(2):
            pool_s[2 * c + k] = dot_nt(
                rounded[:, 256 * k : 256 * k + 256], leaf_blocks(columns[:, 256 * k : 256 * k + 256])
            ).astype(BF)
        return carry

    lax.fori_loop(0, 8, chunk, 0, unroll=2)
    pl.semaphore_wait(barrier, GROUP - 1 + BRANCHES - 1)

    sent = []

    def send(src, dst, send_sem, recv_sem, device_id):
        copy = pltpu.make_async_remote_copy(
            src_ref=src, dst_ref=dst, send_sem=send_sem, recv_sem=recv_sem,
            device_id=device_id, device_id_type=MESH,
        )
        copy.start()
        sent.append(copy)
        return copy

    kept = []

    def keep(src, dst, sem):
        copy = pltpu.make_async_copy(src, dst, sem)
        copy.start()
        kept.append(copy)

    partner_core = (branch, row, 1 - top)
    next_row = (branch, (row + 1) % 4, top)
    last_row = (branch, (row + 3) % 4, top)
    before = ((row + 3) % 4) * 2 + top
    after = ((row + 1) % 4) * 2 + top
    across = ((row + 2) % 4) * 2 + top

    parts = ((0, 16), (16, 16), (32, 32))

    def ring_first(p):
        tiles = pl.ds(*parts[p])
        src = pool_s.at[tiles]
        one = send(src, pool_o.at[me, tiles], ring_send.at[4 * p], ring_recv.at[4 * p], next_row)
        two = send(src, pool_o.at[me, tiles], ring_send.at[4 * p + 1], ring_recv.at[4 * p + 1], last_row)
        core = send(src, pool_o.at[me, tiles], core_send.at[5 * p], core_recv.at[5 * p], partner_core)
        return one, two, core

    def ring_second(p, first):
        tiles = pl.ds(*parts[p])
        first[0].wait_recv()
        lower = pl.ds(parts[p][0], parts[p][1] // 2)
        three = send(
            pool_o.at[before, lower], pool_o.at[before, lower],
            ring_send.at[4 * p + 2], ring_recv.at[4 * p + 2], next_row,
        )
        a = send(
            pool_o.at[before, tiles], pool_o.at[before, tiles],
            core_send.at[5 * p + 1], core_recv.at[5 * p + 1], partner_core,
        )
        first[1].wait_recv()
        higher = pl.ds(parts[p][0] + parts[p][1] // 2, parts[p][1] // 2)
        four = send(
            pool_o.at[after, higher], pool_o.at[after, higher],
            ring_send.at[4 * p + 3], ring_recv.at[4 * p + 3], last_row,
        )
        b = send(
            pool_o.at[after, tiles], pool_o.at[after, tiles],
            core_send.at[5 * p + 2], core_recv.at[5 * p + 2], partner_core,
        )
        return three, four, a, b

    def ring_third(p, second):
        second[0].wait_recv()
        lower = pl.ds(parts[p][0], parts[p][1] // 2)
        a = send(
            pool_o.at[across, lower], pool_o.at[across, lower],
            core_send.at[5 * p + 3], core_recv.at[5 * p + 3], partner_core,
        )
        second[1].wait_recv()
        higher = pl.ds(parts[p][0] + parts[p][1] // 2, parts[p][1] // 2)
        b = send(
            pool_o.at[across, higher], pool_o.at[across, higher],
            core_send.at[5 * p + 4], core_recv.at[5 * p + 4], partner_core,
        )
        return a, b

    first = [ring_first(0)]
    lax.fori_loop(8, 16, chunk, 0, unroll=2)
    first.append(ring_first(1))

    tile_of = [first_row(level) // 4 for level in range(LEVELS)]
    for level in range(LEVELS - 2):
        for t in range((LEAVES >> level) // 8):
            child = tile_of[level] + 2 * t
            pair = jnp.concatenate([pool_s[child], pool_s[child + 1]], axis=1)
            rows = (first_row(level) + 8 * t) * 32
            pool_s[tile_of[level + 1] + t] = dot(pair, edges[rows : rows + 256, :]).astype(BF)
    rows = first_row(5) * 32
    pool_s[63] = dot(pool_s[62], edges[rows : rows + 128, :]).astype(BF)
    rows = first_row(6) * 32
    root = dot(pool_s[63], edges[rows : rows + 128, :])
    placed = root
    for k in (0, 1, 3):
        placed = jnp.where(me % 4 == k, pltpu.roll(root, (32 * (k - 2)) % 128, 1), placed)
    root_s[...] = placed.astype(BF)
    roots = []
    for offset in range(1, GROUP):
        roots.append(
            send(
                root_s, roots_s.at[me],
                root_send.at[offset - 1], root_recv.at[offset - 1], member(peer(offset)),
            )
        )
    roots_s[me] = root_s[...]
    arriving = [first[0][2], first[1][2]]
    fetched[9].wait()
    fetched[10].wait()

    def fill(k, carry):
        for m in range(GROUP):
            near_s[m, k] = table_s[send_s[m, k]]
        for s in range(2):
            side_buf[s, 2 * k] = table_s[side_s[s, 2 * k]]
            side_buf[s, 2 * k + 1] = table_s[side_s[s, 2 * k + 1]]
        return carry

    lax.fori_loop(0, SLOT, fill, 0)

    for offset in range(1, GROUP):
        arriving.append(
            send(
                near_s.at[peer(offset)], table_o.at[pl.ds(me * SLOT, SLOT)],
                near_send.at[offset - 1], near_recv.at[offset - 1], member(peer(offset)),
            )
        )
    arriving.append(
        send(
            side_buf.at[1], table_o.at[pl.ds(LEAVES, HALO)],
            near_send.at[7], near_recv.at[7], cousin(1),
        )
    )
    arriving.append(
        send(
            side_buf.at[0], table_o.at[pl.ds(LEAVES + HALO, HALO)],
            near_send.at[8], near_recv.at[8], cousin(BRANCHES - 1),
        )
    )
    keep(near_s.at[me], table_o.at[pl.ds(me * SLOT, SLOT)], local_sem.at[1])

    first.append(ring_first(2))
    arriving.append(first[2][2])
    keep(pool_s, pool_o.at[me], local_sem.at[2])
    keep(edges, edges_o, local_sem.at[4])

    fetched[5].wait()
    slot = iota((64, 496), 0)
    want = jnp.where(
        slot < 8,
        8 * branch + slot,
        jnp.where(
            slot < 12,
            248 + 4 * branch + slot,
            jnp.where(slot < 14, 372 + 2 * branch + slot, jnp.where(slot < 16, -1, 432 + slot)),
        ),
    )
    chosen = dot((iota((64, 496), 1) == want).astype(F32).astype(BF), tup[...])

    def put_up(p, out):
        edge_s[0, pl.ds(p, 64, stride=PITCH), :] = out

    spread_edges(lambda g: chosen[:, 128 * g : 128 * g + 128], put_up)
    for u in range(64):
        edges_up[32 * u : 32 * u + 32, :] = edge_s[0, PITCH * u : PITCH * u + 32].astype(BF)
    keep(edges_up, edges_up_o, local_sem.at[5])

    for copy in roots:
        copy.wait_recv()
    low = roots_s[0] + roots_s[1] + roots_s[2] + roots_s[3]
    high = roots_s[4] + roots_s[5] + roots_s[6] + roots_s[7]
    upper_s[0] = low
    upper_s[1] = high
    level1 = dot(jnp.concatenate([low, high], axis=1), edges_up[0:256, :]).astype(BF)
    upper_s[2] = level1
    level2 = dot(level1, edges_up[256:384, :]).astype(BF)
    level3 = dot(level2[:, 0:64], edges_up[384:448, :]).astype(BF)
    upper_s[3] = jnp.where(left, level2.astype(F32), level3.astype(F32)).astype(BF)

    def spread_up(offset, carry):
        pltpu.make_async_remote_copy(
            src_ref=upper_s, dst_ref=upper_o.at[branch],
            send_sem=up_send.at[offset - 1], recv_sem=up_recv.at[offset - 1],
            device_id=cousin(offset), device_id_type=MESH,
        ).start()
        return carry

    lax.fori_loop(1, BRANCHES, spread_up, 0)
    keep(upper_s, upper_o.at[branch], local_sem.at[3])

    fetched[6].wait()
    slot = iota((16, 252), 0)
    shape = slot & 7
    base = jnp.where(slot < 8, device, device + 1 - 2 * top)
    node = jnp.full((16, 252), -1, I32)
    for level in range(6):
        node = jnp.where(shape == level, 512 - (512 >> level) + (base >> level), node)
    hot = (iota((16, 252), 1) + 252 * top == node).astype(F32).astype(BF)
    for f in range(FAR):
        chosen = dot(hot, cup[f])
        cup_own[f] = chosen[0:8]
        cup_send[f] = chosen[8:16]
    cup_copy = send(cup_send, cup_recv, cup_sem.at[0], cup_sem.at[1], partner_core)

    fetched[8].wait()
    column = iota((FAR, 254), 1)
    width = jnp.full((FAR, 254), 7, I32)
    start = jnp.zeros((FAR, 254), I32)
    for level in range(1, LEVELS):
        width = jnp.where(column >= first_row(level), 7 - level, width)
        start = jnp.where(column >= first_row(level), first_row(level), start)
    codes[:, 254:256] = jnp.zeros((FAR, 2), I32)
    codes[:, 0:254] = (partner[...] >> width) * 256 + start + (partner[...] & ((1 << width) - 1))
    keep(codes, codes_o, local_sem.at[6])

    second = [ring_second(0, first[0]), ring_second(1, first[1])]
    arriving += second[0][2:] + second[1][2:]

    fetched[7].wait()
    for f in range(FAR):
        block_tail[f] = jnp.zeros((16, 1024), F32)
        block_tail[f, 0:14, :] = couple[f, 240:254, :].astype(F32)

    def couple_one(rows_of, start, part):
        def put(a, low, high):
            block_s[part, 0, pl.ds(a, 16, stride=PITCH), :] = low
            block_s[part, 1, pl.ds(a, 16, stride=PITCH), :] = high

        spread_blocks(rows_of, put)
        for half in range(2):
            for u in range(16):
                rows = pl.ds(pl.multiple_of(start + 32 * u, 32), 32)
                blocks[rows, 128 * half : 128 * half + 128] = block_s[
                    part, half, PITCH * u : PITCH * u + 32
                ].astype(BF)

    def couple_rows(c, carry):
        for part in range(3):
            start = pl.multiple_of(48 * c + 16 * part, 16)
            couple_one(
                lambda f, g: couple[f, pl.ds(start, 16), 128 * g : 128 * g + 128].astype(F32),
                1536 * c + 512 * part, part,
            )
        return carry

    lax.fori_loop(0, 5, couple_rows, 0)
    couple_one(lambda f, g: block_tail[f, :, 128 * g : 128 * g + 128], 7680, 0)
    keep(blocks, blocks_o, local_sem.at[7])
    second.append(ring_second(2, first[2]))
    arriving += second[2][2:]

    eye = (iota((128, 128), 0) == iota((128, 128), 1)).astype(F32).astype(BF)

    def goals(c, carry):
        lanes = pl.ds(pl.multiple_of(c * 128, 128), 128)
        features = target_features(xyz[:, lanes].astype(F32)).astype(BF)
        turned = dot_nt(eye, jnp.concatenate([features] * 4, axis=0)).astype(BF)
        goals_s[2 * c] = turned[0:64]
        goals_s[2 * c + 1] = turned[64:128]
        return carry

    lax.fori_loop(0, 64, goals, 0, unroll=16)
    keep(goals_s, goals_o, local_sem.at[9])
    swap_halves(table_s, swap_s, LEAVES)
    fetched[11].wait()
    fetched[12].wait()

    def own_pairs(c, carry):
        for k in range(16):
            place = 64 * c + 4 * k
            at = [jnp.minimum(source[0, RECEIVED + place + i], LEAVES - 1) for i in range(4)]
            to = [target[0, RECEIVED + place + i] for i in range(4)]
            for i, part in enumerate(near_quad(goals_s, table_s, swap_s, at, to, left)):
                terms[place + i] = part.astype(BF)
        return carry

    for k, (start, stop) in enumerate(((0, 5), (5, 9), (9, 13))):
        lax.fori_loop(start, stop, own_pairs, 0)
        span = pl.ds(64 * start, 64 * (stop - start))
        keep(terms.at[span], terms_o.at[span], local_sem.at[10 + k])
        arriving += ring_third(k, second[k])

    cup_copy.wait_recv()
    cup_own[...] = cup_own[...] + cup_recv[...]
    keep(cup_own, cup_o, local_sem.at[8])
    for copy in arriving:
        copy.wait_recv()
    for copy in sent:
        copy.wait_send()

    def finish(offset, carry):
        pltpu.make_async_remote_copy(
            src_ref=upper_s, dst_ref=upper_o.at[branch],
            send_sem=up_send.at[offset - 1], recv_sem=up_recv.at[offset - 1],
            device_id=cousin(offset), device_id_type=MESH,
        ).wait()
        return carry

    lax.fori_loop(1, BRANCHES, finish, 0)
    for copy in kept:
        copy.wait()


def exchange(rhs, xyz, order, basis, trans, tup, cup, couple, partner, send_list, side_list, target, source):
    shape = jax.ShapeDtypeStruct
    inputs = (rhs, xyz, order, basis, trans, tup, cup, couple, partner, send_list, side_list, target, source)
    return pl.pallas_call(
        exchange_kernel,
        out_shape=(
            shape((RECEIVED, 16, 128), BF),
            shape((GROUP, TILES, 16, 128), BF),
            shape((BRANCHES, 4, 16, 128), BF),
            shape((8192, 128), BF),
            shape((2048, 128), BF),
            shape((FAR, 8, 1024), F32),
            shape((8192, 256), BF),
            shape((FAR, 256), I32),
            shape((LEAVES, 64, 64), BF),
            shape((OWN, 16, 64), BF),
        ),
        in_specs=[HBM] * 13,
        out_specs=(HBM,) * 10,
        scratch_shapes=[pltpu.VMEM(value.shape, value.dtype) for value in inputs[:9]]
        + [pltpu.SMEM(value.shape, value.dtype) for value in inputs[9:]]
        + [
            pltpu.VMEM((512, 256), BF),
            pltpu.VMEM((LEAVES, 16, 128), BF),
            pltpu.VMEM((TILES, 16, 128), BF),
            pltpu.VMEM((3, 64 * PITCH, 128), F32),
            pltpu.VMEM((16, 1024), F32),
            pltpu.VMEM((GROUP, SLOT, 16, 128), BF),
            pltpu.VMEM((2, HALO, 16, 128), BF),
            pltpu.VMEM((16, 128), BF),
            pltpu.VMEM((GROUP, 16, 128), BF),
            pltpu.VMEM((4, 16, 128), BF),
            pltpu.VMEM((FAR, 8, 1024), F32),
            pltpu.VMEM((FAR, 8, 1024), F32),
            pltpu.VMEM((FAR, 8, 1024), F32),
            pltpu.VMEM((8192, 128), BF),
            pltpu.VMEM((2048, 128), BF),
            pltpu.VMEM((3, 2, 16 * PITCH, 128), F32),
            pltpu.VMEM((FAR, 16, 1024), F32),
            pltpu.VMEM((8192, 256), BF),
            pltpu.VMEM((FAR, 256), I32),
            pltpu.VMEM((LEAVES, 64, 64), BF),
            pltpu.VMEM((LEAVES, 16, 128), BF),
            pltpu.VMEM((OWN, 16, 64), BF),
        ]
        + [
            pltpu.SemaphoreType.DMA((count,))
            for count in (13, 9, 9, 15, 15, 12, 12, 7, 7, BRANCHES - 1, BRANCHES - 1, 2, 13)
        ],
        compiler_params=pltpu.CompilerParams(
            collective_id=0, has_side_effects=True, vmem_limit_bytes=64 * 1024 * 1024
        ),
        name="exchange",
    )(*inputs)


def local_kernel(
    table_h, target_h, source_h, count_h, goals_h, terms_h, pool_h, blocks_h, codes_h, upper_h, edges_up_h, cup_h, pup_h,
    edges_h, basis_h, order_h,
    out,
    table, target, source, count, goals, terms, pool, blocks, codes, upper, edges_up, cup, pup, edges, basis, order,
    swap_s, pool_rep, block_up, upper_s, coupled_s, local_s, near_s, sum_s, in_sem,
):
    given = (table_h, target_h, source_h, count_h, goals_h, terms_h, pool_h, blocks_h, codes_h, upper_h, edges_up_h, cup_h, pup_h,
             edges_h, basis_h, order_h)
    held = (table, target, source, count, goals, terms, pool, blocks, codes, upper, edges_up, cup, pup, edges, basis, order)
    fetched = [pltpu.make_async_copy(a, b, in_sem.at[i]) for i, (a, b) in enumerate(zip(given, held))]
    for copy in fetched:
        copy.start()
    branch = lax.axis_index("branch")
    me = lax.axis_index("row") * 2 + lax.axis_index("top")
    device = branch * GROUP + me
    left = iota((16, 128), 1) < 64
    lane_block = iota((16, 128), 1) >> 5

    def clear(t, carry):
        near_s[t] = jnp.zeros((16, 64), F32)
        return carry

    lax.fori_loop(0, LEAVES + 1, clear, 0, unroll=3)

    for copy in fetched[:5]:
        copy.wait()
    swap_halves(table, swap_s, RECEIVED)
    zero = jnp.zeros((16, 128), BF)

    def near(c, carry):
        outs = []
        for k in range(16):
            place = 64 * c + 4 * k
            at = [source[0, place + i] - LEAVES for i in range(4)]
            to = [target[0, place + i] for i in range(4)]
            outs += zip(to, near_quad(goals, table, swap_s, at, to, left))
        for goal, part in outs:
            near_s[goal] = near_s[goal] + part
        return carry

    lax.fori_loop(0, RECEIVED // 64, near, 0)
    fetched[5].wait()
    live = count[0] - RECEIVED

    def add_terms(c, carry):
        for k in range(16):
            place = 16 * c + k
            goal = jnp.where(place < live, target[0, RECEIVED + place], LEAVES)
            near_s[goal] = near_s[goal] + terms[place].astype(F32)
        return carry

    lax.fori_loop(0, (live + 15) // 16, add_terms, 0)

    for copy in fetched[6:13]:
        copy.wait()

    def put_up(a, low, high):
        block_up[0, pl.ds(a, 8, stride=32), :] = low
        block_up[1, pl.ds(a, 8, stride=32), :] = high

    spread_blocks(lambda f, g: cup[f, :, 128 * g : 128 * g + 128], put_up)

    wide_block = iota((128, 128), 1) >> 5

    def widen(t, carry):
        tiles = pool[pl.ds(8 * t, 8)].reshape(128, 128).astype(F32)
        turns = [v.astype(BF) for v in block_turns(tiles)]
        for j in range(4):
            value = turns[(3 - j) % 4]
            for k in range(3):
                value = jnp.where(wide_block == k, turns[(k - j) % 4], value)
            pool_rep[pl.ds(8 * t, 8), j] = value.reshape(8, 16, 128)
        return carry

    lax.fori_loop(0, GROUP * TILES // 8, widen, 0, unroll=4)

    def picks_of(pick):
        low = jnp.where(
            lane_block == 0,
            pick[0],
            jnp.where(lane_block == 1, pick[1], jnp.where(lane_block == 2, pick[2], pick[3])),
        )
        high = jnp.where(lane_block == 0, pick[4], jnp.where(lane_block == 1, pick[5], zero))
        return jnp.concatenate([low, high], axis=1)

    def diagonal(wide):
        tiles = []
        for half in range(2):
            tile = wide[64 * half + 48 : 64 * half + 64, 128 * half : 128 * half + 128]
            for j in range(3):
                start = 64 * half + 16 * j
                tile = jnp.where(
                    lane_block == j, wide[start : start + 16, 128 * half : 128 * half + 128], tile
                )
            tiles.append(tile)
        return tiles

    def coupling(c, carry):
        rows = []
        for u in range(8):
            rows.append(picks_of([pool_rep[codes[f, 8 * c + u] >> 2, codes[f, 8 * c + u] & 3] for f in range(FAR)]))
        matrices = blocks[pl.ds(pl.multiple_of(c * 256, 256), 256), :]
        tiles = diagonal(dot_nt(jnp.concatenate(rows, axis=0), matrices))
        coupled_s[2 * c] = tiles[0]
        coupled_s[2 * c + 1] = tiles[1]
        return carry

    lax.fori_loop(0, 32, coupling, 0, unroll=4)

    def thirds(t, carry):
        tile = jnp.zeros((16, 128), F32)
        for j in range(4):
            tile = jnp.where(
                lane_block == j, pltpu.roll(upper[4 * t + j, 3].astype(F32), (32 * (j - 2)) % 128, 1), tile
            )
        upper_s[t] = tile.astype(BF)
        return carry

    lax.fori_loop(0, 8, thirds, 0)
    for t in range(4):
        pair = jnp.concatenate([upper_s[2 * t], upper_s[2 * t + 1]], axis=1)
        upper_s[8 + t] = dot(pair, edges_up[512 + 256 * t : 768 + 256 * t, :]).astype(BF)
    for t in range(2):
        pair = jnp.concatenate([upper_s[8 + 2 * t], upper_s[9 + 2 * t]], axis=1)
        upper_s[12 + t] = dot(pair, edges_up[1536 + 256 * t : 1792 + 256 * t, :]).astype(BF)

    def everywhere(tile, block):
        only = jnp.where(lane_block == block, tile, 0.0)
        only = only + pltpu.roll(only, 32, 1)
        return only + pltpu.roll(only, 64, 1)

    rows = []
    for level in range(6):
        node = 512 - (512 >> level) + (device >> level)
        pick = []
        for f in range(FAR):
            q = pup[f, node] - (512 - (512 >> level))
            if level == 0:
                tile, block = upper[q >> 3, (q >> 2) & 1], q & 3
            elif level == 1:
                tile, block = upper[q >> 2, 2], q & 3
            elif level == 2:
                tile, block = upper[q >> 1, 3], q & 1
            elif level == 3:
                tile, block = upper[q, 3], 2
            else:
                tile, block = upper_s[(8 if level == 4 else 12) + (q >> 2)], q & 3
            pick.append(everywhere(tile.astype(F32), block).astype(BF))
        rows.append(picks_of(pick))
    rows += [jnp.zeros((16, 256), BF)] * 2
    tiles = diagonal(dot_nt(jnp.concatenate(rows, axis=0), jnp.concatenate([block_up[0], block_up[1]], axis=1).astype(BF)))
    edge_rows = [me, 8 + (me >> 1), 12 + (me >> 2), 16 + branch, 48 + (branch >> 1)]
    current = everywhere(tiles[1], 1)
    for level in range(4, -1, -1):
        matrix = edges_up[pl.ds(pl.multiple_of(edge_rows[level] * 32, 32), 32), :]
        step = dot_nt(current.astype(BF), jnp.concatenate([matrix] * 4, axis=0))
        current = everywhere(tiles[level // 4], level % 4) + step

    for copy in fetched[13:]:
        copy.wait()
    rows6 = first_row(6) * 32
    local_s[63] = coupled_s[63] + dot_nt(current.astype(BF), edges[rows6 : rows6 + 128, :])
    rows5 = first_row(5) * 32
    local_s[62] = coupled_s[62] + dot_nt(local_s[63].astype(BF), edges[rows5 : rows5 + 128, :])
    for level in range(LEVELS - 3, -1, -1):
        parent = first_row(level + 1) // 4
        child = first_row(level) // 4
        for t in range((LEAVES >> level) // 8):
            start = (first_row(level) + 8 * t) * 32
            wide = dot_nt(local_s[parent + t].astype(BF), edges[start : start + 256, :])
            local_s[child + 2 * t] = coupled_s[child + 2 * t] + wide[:, 0:128]
            local_s[child + 2 * t + 1] = coupled_s[child + 2 * t + 1] + wide[:, 128:256]

    sum_s[...] = jnp.zeros((512, 256), F32)

    def back(c, carry):
        tall, hots = [], []
        lows = []
        for k in range(4):
            lanes = pl.ds(pl.multiple_of((4 * c + k) * 256, 256), 256)
            far = dot(local_s[4 * c + k].astype(BF), leaf_blocks(basis[:, lanes]))
            parts = []
            for half in range(2):
                first = near_s[16 * c + 4 * k + 2 * half]
                second = near_s[16 * c + 4 * k + 2 * half + 1]
                parts += [first, second]
            tall.append((far + INV_FOUR_PI * jnp.concatenate(parts, axis=1)).astype(BF))
            index = order[:, lanes]
            lows.append(jnp.broadcast_to((index >> 8).astype(F32), (16, 256)).astype(BF))
            fine = jnp.broadcast_to((index & 255).astype(F32), (16, 256)).astype(BF)
            fine = jnp.concatenate([fine] * 16, axis=0)
            hots.append(jnp.where(row_id == fine, jnp.ones((), BF), jnp.zeros((), BF)))
        total = jnp.concatenate(tall, axis=1)
        part = jnp.concatenate(lows, axis=1)
        none = jnp.zeros((16, 1024), BF)
        rows = jnp.concatenate(
            [jnp.where(part == jnp.asarray(low, BF), total, none) for low in range(32)], axis=0
        )
        sum_s[...] += dot_nt(rows, jnp.concatenate(hots, axis=1))
        return carry

    row_id = iota((256, 256), 0).astype(F32).astype(BF)
    lax.fori_loop(0, 8, back, 0)
    for low in range(32):
        out[:, 256 * low : 256 * low + 256] = sum_s[16 * low : 16 * low + 16, :]


def local(*inputs):
    scalars = (1, 2, 3, 8, 12)
    return pl.pallas_call(
        local_kernel,
        out_shape=jax.ShapeDtypeStruct((NRHS, POINTS), F32),
        in_specs=[HBM] * 16,
        out_specs=VMEM,
        scratch_shapes=[
            (pltpu.SMEM if i in scalars else pltpu.VMEM)(value.shape, value.dtype) for i, value in enumerate(inputs)
        ]
        + [
            pltpu.VMEM((RECEIVED, 16, 128), BF),
            pltpu.VMEM((GROUP * TILES, 4, 16, 128), BF),
            pltpu.VMEM((2, 256, 128), F32),
            pltpu.VMEM((14, 16, 128), BF),
            pltpu.VMEM((TILES, 16, 128), F32),
            pltpu.VMEM((TILES, 16, 128), F32),
            pltpu.VMEM((LEAVES + 1, 16, 64), F32),
            pltpu.VMEM((512, 256), F32),
            pltpu.SemaphoreType.DMA((16,)),
        ],
        compiler_params=pltpu.CompilerParams(vmem_limit_bytes=64 * 1024 * 1024),
        name="local",
    )(*inputs)


def body(
    right_sides,
    positions,
    point_order,
    leaf_basis,
    transfer,
    couple_local,
    partner_local,
    transfer_up,
    couple_up,
    partner_up,
    send_list,
    side_list,
    pair_target,
    pair_source,
    pair_count,
):
    order = point_order.reshape(1, POINTS)
    table, pool, upper, edges, edges_up, cup, blocks, codes, goals, terms = exchange(
        right_sides, positions, order, leaf_basis, transfer, transfer_up,
        couple_up.transpose(1, 0, 2), couple_local.transpose(1, 0, 2), partner_local.T, send_list[0], side_list[0],
        pair_target, pair_source,
    )
    return local(
        table, pair_target, pair_source, pair_count, goals, terms, pool.reshape(GROUP * TILES, 16, 128), blocks, codes,
        upper, edges_up, cup, partner_up.T, edges, leaf_basis, order,
    )


def solution(mesh):
    placed = (
        P(None, ("branch", "row", "top")),
        P(None, ("branch", "row", "top")),
        P(("branch", "row", "top")),
        P(None, ("branch", "row", "top")),
        P(("branch", "row", "top"), None),
        P(("branch", "row", "top"), None, None),
        P(("branch", "row", "top"), None),
        P(),
        P("top", None, None),
        P(),
        P(("branch", "row", "top"), None, None),
        P(("branch", "row", "top"), None, None),
        P(("branch", "row", "top"), None),
        P(("branch", "row", "top"), None),
        P(("branch", "row", "top")),
    )
    return jax.shard_map(
        body,
        mesh=mesh,
        in_specs=placed,
        out_specs=P(None, ("branch", "row", "top")),
        check_vma=False,
    )
```
